512 devices in a mesh: tm: 32 (over x, z_lo), clip: 16 (over z_hi, y, core).
Axes of the slice: x: 4, y: 4, z: 16 (z_hi: 2, z_lo: 8; z = z_hi * 8 + z_lo), core: 2. Of those that a mesh axis runs over, the one named last changes fastest.
Arguments:
- video: float32 [16, 32, 16, 32, 320], P('clip', 'tm'), may hold values from -6 to 6
- spatial_w: bfloat16 [9, 320, 320], P(None, 'clip'), may hold values from -0.109375 to 0.109375
- spatial_b: float32 [320], replicated, may hold values from -3 to 3
- temporal_w: float32 [3, 320, 320], P(None, 'clip'), may hold values from -0.1875 to 0.1875
- cotangent: float32 [16, 32, 16, 32, 320], P('clip', 'tm'), may hold values from -6 to 6
Outputs:
- output: float32 [16, 32, 16, 32, 320], P('clip', 'tm')
- grad_video: float32 [16, 32, 16, 32, 320], P('clip', 'tm')
- grad_temporal: float32 [3, 320, 320], P(None, 'clip')
The draws below stay inside these ranges and needn't reach their ends.
All inputs are finite; a program needn't handle non-finite values.
Results may differ from the reference program's by a relative error of at most 0.0049.
Values may be sent and summed in bfloat16 or wider, within the bound.
No kernel may reach another device: no remote copies, remote signals or barrier semaphores. Data moves between devices by JAX's collectives and lax.ppermute only.
A program may use at most 64 MiB of HBM per device.

```python
import math
import jax
import jax.numpy as jnp
from jax import lax

C = 320
HEIGHT = 16
WIDTH = 32
FRAMES = 32
CLIPS = 16
ROWS_ALL = 262144


def steps_of(rng, extent, split, low, high):
    gain, own = 1.0, jax.random.fold_in(rng, 6)
    for axis_at, blocks in split:
        draws = jnp.exp(jax.random.uniform(jax.random.fold_in(own, axis_at), (blocks,), jnp.float32, low / len(split), high / len(split)))
        gain = gain * jnp.repeat(draws, extent[axis_at] // blocks).reshape([-1 if axis == axis_at else 1 for axis in range(len(extent))])
    return gain


def bell_draw(key, extent, deviation, bound, shards=(), kind=jnp.bfloat16):
    values = deviation * jax.random.normal(key, extent, jnp.float32)
    if shards:
        values = values * steps_of(key, extent, shards, -0.22, 0.18)
    return jnp.clip(values, -bound, bound).astype(kind)


def setup_inputs(seed: int = 0) -> dict:
    splits = jax.random.split(jax.random.key(seed), 6)
    video = bell_draw(splits[0], (CLIPS, FRAMES, HEIGHT, WIDTH, C), 1.0, 6.0, ((0, 16), (1, 32)), jnp.float32)
    spatial_w = bell_draw(splits[1], (9, C, C), (9 * C) ** -0.5, 0.109375, ((1, 16),))
    spatial_b = bell_draw(splits[2], (C,), 0.5, 3.0, (), jnp.float32)
    temporal_w = bell_draw(splits[3], (3, C, C), (3 * C) ** -0.5, 0.1875, ((1, 16),), jnp.float32)
    cotangent = bell_draw(splits[4], (CLIPS, FRAMES, HEIGHT, WIDTH, C), 1.0, 6.0, ((0, 16), (1, 32)), jnp.float32)
    return {"video": video, "spatial_w": spatial_w, "spatial_b": spatial_b, "temporal_w": temporal_w, "cotangent": cotangent}


def outer_dot(left, right):
    return lax.dot_general(left, right, (((0,), (0,)), ((), ())), preferred_element_type=jnp.float32)

def transpose_dot(left, right):
    return lax.dot_general(left, right, (((1,), (1,)), ((), ())), preferred_element_type=jnp.float32)

def one_clip(video, cotangent, spatial_w, spatial_b, temporal_b):
    frames, height, width, chans = video.shape
    row_count = frames * height * width
    video_b = video.astype(jnp.bfloat16)
    padded = jnp.pad(video_b, ((0, 0), (1, 1), (1, 1), (0, 0)))
    spatial = jnp.zeros((row_count, chans), jnp.float32)
    for shift_y in range(3):
        for shift_x in range(3):
            columns = padded[:, shift_y:shift_y + height, shift_x:shift_x + width, :].reshape(row_count, chans)
            spatial = spatial + jnp.dot(columns, spatial_w[3 * shift_y + shift_x], preferred_element_type=jnp.float32)
    spatial = spatial + spatial_b
    sigmoid_s = jax.nn.sigmoid(spatial)
    hidden = (spatial * sigmoid_s).astype(jnp.bfloat16).reshape(frames, height, width, chans)
    hidden_pad = jnp.pad(hidden, ((1, 1), (0, 0), (0, 0), (0, 0)))
    temporal = jnp.zeros((row_count, chans), jnp.float32)
    for kernel_tap in range(3):
        shifted = hidden_pad[kernel_tap:kernel_tap + frames].reshape(row_count, chans)
        temporal = temporal + jnp.dot(shifted, temporal_b[kernel_tap], preferred_element_type=jnp.float32)
    output = video + temporal.reshape(video.shape)
    cot_b = cotangent.astype(jnp.bfloat16)
    cot_flat = cot_b.reshape(row_count, chans)
    cot_pad = jnp.pad(cot_b, ((1, 1), (0, 0), (0, 0), (0, 0)))
    grad_hidden = jnp.zeros((row_count, chans), jnp.float32)
    grads = []
    for kernel_tap in range(3):
        shifted_cot = cot_pad[2 - kernel_tap:2 - kernel_tap + frames].reshape(row_count, chans)
        grad_hidden = grad_hidden + transpose_dot(shifted_cot, temporal_b[kernel_tap])
        shifted_hid = hidden_pad[kernel_tap:kernel_tap + frames].reshape(row_count, chans)
        grads.append(outer_dot(shifted_hid, cot_flat))
    grad_spatial = (grad_hidden * sigmoid_s * (1.0 + spatial * (1.0 - sigmoid_s))).astype(jnp.bfloat16)
    grad_pad = jnp.zeros((frames, height + 2, width + 2, chans), jnp.float32)
    for shift_y in range(3):
        for shift_x in range(3):
            contrib = transpose_dot(grad_spatial, spatial_w[3 * shift_y + shift_x]).reshape(frames, height, width, chans)
            grad_pad = grad_pad.at[:, shift_y:shift_y + height, shift_x:shift_x + width, :].add(contrib)
    grad_video = cotangent + grad_pad[:, 1:-1, 1:-1, :]
    return (output, grad_video, jnp.stack(grads))

def reference(video, spatial_w, spatial_b, temporal_w, cotangent):
    temporal_b = temporal_w.astype(jnp.bfloat16)

    def per_clip(pair):
        return one_clip(pair[0], pair[1], spatial_w, spatial_b, temporal_b)
    output, grad_video, grads = lax.map(per_clip, (video, cotangent))
    grad_temporal = lax.optimization_barrier(jnp.sum(grads, axis=0)) * (1.0 / math.sqrt(ROWS_ALL))
    return (output, grad_video, grad_temporal)
```

```python
import math

import jax
import jax.numpy as jnp
from jax import lax
from jax.experimental import pallas as pl
from jax.experimental.pallas import tpu as pltpu
from jax.sharding import Mesh
from jax.sharding import PartitionSpec as P

AXES = ("x", "m", "k", "h", "y", "c")
SIZES = (4, 2, 4, 2, 4, 2)
TM = ("x", "m", "k")
Z_LO = ("m", "k")
CLIP = ("h", "y", "c")
PLANE = ("x", "y")
H, W, C = 16, 32, 320
ROWS = H * W
HALF, PART, OWN = 160, 40, 20
TAPS = 12
PIECE = 64
BF = jnp.bfloat16
F32 = jnp.float32


def pairs_across():
    def place(z):
        return (z % 8) * 2 + z // 8

    there = [(z - 4) % 16 if z % 8 < 4 else (z + 4) % 16 for z in range(16)]
    return [(place(z), place(there[z])) for z in range(16)]


ACROSS = pairs_across()
FRAMES_UP = [(t, t + 1) for t in range(31)]
FRAMES_DOWN = [(t + 1, t) for t in range(31)]


def across(a):
    return lax.ppermute(a, ("m", "k", "h"), ACROSS)


def core_swap(a):
    return lax.ppermute(a, "c", [(0, 1), (1, 0)])


def to_all(a, axes):
    n = lax.axis_size(axes)
    return lax.all_to_all(jnp.broadcast_to(a[None], (n, *a.shape)), axes, 0, 0, tiled=True)


def start_of(x):
    return min(PIECE * x, 6 * PART - PIECE)


def dot(a, b):
    return lax.dot_general(a, b, (((1,), (0,)), ((), ())), preferred_element_type=F32)


def dot_nt(a, b):
    return lax.dot_general(a, b, (((1,), (1,)), ((), ())), preferred_element_type=F32)


def dot_tn(a, b):
    return lax.dot_general(a, b, (((0,), (0,)), ((), ())), preferred_element_type=F32)


def fill_windows(windows, value):
    col = lax.broadcasted_iota(jnp.int32, (ROWS, 1), 0) % W
    edge = jnp.zeros((W, C), BF)
    for d in range(3):
        windows[d, 0:W, :] = edge
        windows[d, W + ROWS : 2 * W + ROWS, :] = edge
    windows[1, W : W + ROWS, :] = value.astype(BF)
    left = jnp.where(col == 0, 0.0, pltpu.roll(value, 1, 0))
    windows[0, W : W + ROWS, :] = left.astype(BF)
    right = jnp.where(col == W - 1, 0.0, pltpu.roll(value, ROWS - 1, 0))
    windows[2, W : W + ROWS, :] = right.astype(BF)


def tap(w_ref, t):
    return w_ref[t].reshape(C, C)


def forward_kernel(
    place, own_m, own_t, oth_m, oth_t, video, bias, cot, cot_prev, cot_next,
    w_ref, hidden_ref, slope_ref, mine_ref, theirs_ref, windows,
):
    c, h = place[0], place[1]
    for source, first, half in (
        (own_m, 6 * c, h), (own_t, 6 * (1 - c), h),
    ):
        for y in range(4):
            for t in range(6):
                w_ref[first + t, half, y * PART : (y + 1) * PART, :] = source[y, t * PART : (t + 1) * PART, :]
    for source, first, half in (
        (oth_m, 6 * c, 1 - h), (oth_t, 6 * (1 - c), 1 - h),
    ):
        for x in range(4):
            for y in range(4):
                at, stop = PIECE * x, min(PIECE * (x + 1), 6 * PART)
                while at < stop:
                    t, r = divmod(at, PART)
                    n = min(PART - r, stop - at)
                    s = at - start_of(x)
                    w_ref[first + t, half, y * PART + r : y * PART + r + n, :] = source[x * 4 + y, s : s + n, :]
                    at += n
    fill_windows(windows, video[...])
    spatial = jnp.zeros((ROWS, C), F32) + bias[...]
    for a in range(3):
        for b in range(3):
            spatial = spatial + dot(windows[b, a * W : a * W + ROWS, :], tap(w_ref, 3 * a + b))
    sig = jax.nn.sigmoid(spatial)
    hidden = (spatial * sig).astype(BF)
    hidden_ref[...] = hidden
    slope_ref[...] = sig * (1.0 + spatial * (1.0 - sig))
    grads = [
        dot_tn(hidden, other)
        for other in (cot_next[...], cot[...].astype(BF), cot_prev[...])
    ]
    pad = jnp.zeros((4, C), F32)
    for half in range(2):
        for y in range(4):
            both = []
            for core in range(2):
                r = half * HALF + y * PART + core * OWN
                both.append(jnp.concatenate([g[r : r + OWN, :] for g in grads] + [pad], axis=0))
            mine = jnp.where(c == 0, both[0], both[1])
            theirs = jnp.where(c == 0, both[1], both[0])
            for x in range(4):
                mine_ref[x, y, half] = mine[16 * x : 16 * x + 16, :]
                theirs_ref[x, y, half] = theirs[16 * x : 16 * x + 16, :]


def backward_kernel(w_ref, slope, cot, cot_prev, cot_next, grad_ref, windows):
    gh = dot_nt(cot_next[...], tap(w_ref, 9))
    gh = gh + dot_nt(cot[...].astype(BF), tap(w_ref, 10))
    gh = gh + dot_nt(cot_prev[...], tap(w_ref, 11))
    gs = (gh * slope[...]).astype(BF).astype(F32)
    fill_windows(windows, gs)
    acc = cot[...]
    for a in range(3):
        for b in range(3):
            acc = acc + dot_nt(windows[2 - b, (2 - a) * W : (2 - a) * W + ROWS, :], tap(w_ref, 3 * a + b))
    grad_ref[...] = acc


def output_kernel(w_ref, video, hidden, prev, after, out_ref):
    acc = video[...] + dot(hidden[...], tap(w_ref, 1))
    acc = acc + dot(prev[...], tap(w_ref, 0))
    out_ref[...] = acc + dot(after[...], tap(w_ref, 2))


def vmem(n):
    return [pl.BlockSpec(memory_space=pltpu.VMEM)] * n


def params():
    return pltpu.CompilerParams(vmem_limit_bytes=48 * 1024 * 1024)


def cost(dots, read):
    return pl.CostEstimate(flops=dots * 2 * ROWS * C * C, bytes_accessed=read, transcendentals=0)


def on_device(video, spatial_w, spatial_b, temporal_w, cotangent):
    c, h, x = lax.axis_index("c"), lax.axis_index("h"), lax.axis_index("x")
    shape = video.shape
    video_f = video.reshape(ROWS, C)
    cot_f = cotangent.reshape(ROWS, C)
    cot_b = cot_f.astype(BF)

    w = jnp.concatenate([spatial_w, temporal_w.astype(BF)], axis=0)
    w = lax.all_to_all(w, "c", 0, 1, tiled=True).reshape(6 * PART, C)
    quarter = lax.dynamic_slice_in_dim(w, jnp.minimum(PIECE * x, 6 * PART - PIECE), PIECE, 0)
    other = across(quarter)
    other, w = lax.optimization_barrier((other, w))
    own_m = to_all(w, "y")
    oth_m = to_all(other, PLANE)
    cot_next = lax.ppermute(cot_b, TM, FRAMES_DOWN)
    cot_prev = lax.ppermute(cot_b, TM, FRAMES_UP)
    own_t, oth_t = core_swap(own_m), core_swap(oth_m)

    place = jnp.stack([c, h]).astype(jnp.int32)
    w_all, hidden, slope, mine, theirs = pl.pallas_call(
        forward_kernel,
        out_shape=(
            jax.ShapeDtypeStruct((TAPS, 2, HALF, C), BF),
            jax.ShapeDtypeStruct((ROWS, C), BF),
            jax.ShapeDtypeStruct((ROWS, C), F32),
            jax.ShapeDtypeStruct((4, 4, 2, 16, C), F32),
            jax.ShapeDtypeStruct((4, 4, 2, 16, C), F32),
        ),
        in_specs=[pl.BlockSpec(memory_space=pltpu.SMEM)] + vmem(9),
        out_specs=vmem(5),
        scratch_shapes=[pltpu.VMEM((3, ROWS + 2 * W, C), BF)],
        compiler_params=params(),
        cost_estimate=cost(12, 8_000_000),
        name="forward",
    )(place, own_m, own_t, oth_m, oth_t, video_f, spatial_b.reshape(1, C), cot_f, cot_prev, cot_next)

    part = mine + core_swap(theirs)
    part = lax.all_to_all(part.reshape(16, 2, 16, C), PLANE, 0, 0, tiled=True)

    prev = lax.ppermute(hidden, TM, FRAMES_UP)
    after = lax.ppermute(hidden, TM, FRAMES_DOWN)
    grad_video = pl.pallas_call(
        backward_kernel,
        out_shape=jax.ShapeDtypeStruct((ROWS, C), F32),
        in_specs=vmem(5),
        out_specs=vmem(1)[0],
        scratch_shapes=[pltpu.VMEM((3, ROWS + 2 * W, C), BF)],
        compiler_params=params(),
        cost_estimate=cost(12, 5_000_000),
        name="backward",
    )(w_all, slope, cot_f, cot_prev, cot_next)

    part = jnp.sum(part, axis=0)
    keep = jnp.where(h == 0, part[0], part[1])
    give = jnp.where(h == 0, part[1], part[0])
    part = keep + across(give)
    part = jnp.sum(to_all(part, Z_LO), axis=0)
    part = to_all(part, "x").reshape(4 * 16, C)
    output = pl.pallas_call(
        output_kernel,
        out_shape=jax.ShapeDtypeStruct((ROWS, C), F32),
        in_specs=vmem(5),
        out_specs=vmem(1)[0],
        compiler_params=params(),
        cost_estimate=cost(3, 3_000_000),
        name="output",
    )(w_all[9:], video_f, hidden, prev, after)
    total_rows = ROWS * lax.axis_size(TM) * lax.axis_size(CLIP)
    grad_temporal = part[: 3 * OWN].reshape(3, OWN, C) * (1.0 / math.sqrt(total_rows))
    return output.reshape(shape), grad_video.reshape(shape), grad_temporal


def solution(mesh):
    finer = Mesh(mesh.devices.reshape(SIZES), AXES)
    placed = (
        P(CLIP, TM, None, None, None),
        P(None, CLIP, None),
        P(),
        P(None, CLIP, None),
        P(CLIP, TM, None, None, None),
    )
    return jax.shard_map(
        on_device,
        mesh=finer,
        in_specs=placed,
        out_specs=(
            P(CLIP, TM, None, None, None),
            P(CLIP, TM, None, None, None),
            P(None, CLIP, None),
        ),
        check_vma=False,
    )
```

```python
import math

import jax
import jax.numpy as jnp
from jax import lax
from jax.experimental import pallas as pl
from jax.experimental.pallas import tpu as pltpu
from jax.sharding import Mesh
from jax.sharding import PartitionSpec as P

AXES = ("x", "m", "k", "h", "y", "c")
SIZES = (4, 2, 4, 2, 4, 2)
TM = ("x", "m", "k")
Z_LO = ("m", "k")
CLIP = ("h", "y", "c")
PLANE = ("x", "y")
H, W, C = 16, 32, 320
ROWS = H * W
HALF, PART, OWN = 160, 40, 20
TAPS = 12
BF = jnp.bfloat16
F32 = jnp.float32


def pairs_across():
    def place(z):
        return (z % 8) * 2 + z // 8

    there = [(z - 4) % 16 if z % 8 < 4 else (z + 4) % 16 for z in range(16)]
    return [(place(z), place(there[z])) for z in range(16)]


ACROSS = pairs_across()
FRAMES_UP = [(t, t + 1) for t in range(31)]
FRAMES_DOWN = [(t + 1, t) for t in range(31)]


def across(a):
    return lax.ppermute(a, ("m", "k", "h"), ACROSS)


def core_swap(a):
    return lax.ppermute(a, "c", [(0, 1), (1, 0)])


def to_all(a, axes):
    n = lax.axis_size(axes)
    return lax.all_to_all(jnp.broadcast_to(a[None], (n, *a.shape)), axes, 0, 0, tiled=True)


def dot(a, b):
    return lax.dot_general(a, b, (((1,), (0,)), ((), ())), preferred_element_type=F32)


def dot_nt(a, b):
    return lax.dot_general(a, b, (((1,), (1,)), ((), ())), preferred_element_type=F32)


def dot_tn(a, b):
    return lax.dot_general(a, b, (((0,), (0,)), ((), ())), preferred_element_type=F32)


def fill_windows(windows, value):
    col = lax.broadcasted_iota(jnp.int32, (ROWS, 1), 0) % W
    edge = jnp.zeros((W, C), BF)
    for d in range(3):
        windows[d, 0:W, :] = edge
        windows[d, W + ROWS : 2 * W + ROWS, :] = edge
    windows[1, W : W + ROWS, :] = value.astype(BF)
    left = jnp.where(col == 0, 0.0, pltpu.roll(value, 1, 0))
    windows[0, W : W + ROWS, :] = left.astype(BF)
    right = jnp.where(col == W - 1, 0.0, pltpu.roll(value, ROWS - 1, 0))
    windows[2, W : W + ROWS, :] = right.astype(BF)


def tap(w_ref, t):
    return w_ref[t].reshape(C, C)


def join(w_ref, t, half, y, mine, theirs, c):
    low = jnp.where(c == 0, mine, theirs)
    high = jnp.where(c == 0, theirs, mine)
    w_ref[t, half, y * PART : (y + 1) * PART, :] = jnp.concatenate([low, high], axis=0)


def prepare_kernel(place, own_m, own_t, video, w_ref, windows):
    c = place[0]
    for t in range(TAPS):
        for y in range(4):
            join(w_ref, t, 0, y, own_m[y, t], own_t[y, t], c)
    fill_windows(windows, video[...])


def forward_kernel(
    place, own, oth_m, oth_t, windows, bias, cot, cot_prev, cot_next,
    w_ref, hidden_ref, slope_ref, mine_ref, theirs_ref,
):
    c, h = place[0], place[1]
    for t in range(TAPS):
        w_ref[t, h] = own[t, 0]
        for y in range(4):
            source = (t // 3) * 4 + y
            join(w_ref, t, 1 - h, y, oth_m[source, t % 3], oth_t[source, t % 3], c)
    spatial = jnp.zeros((ROWS, C), F32) + bias[...]
    for a in range(3):
        for b in range(3):
            spatial = spatial + dot(windows[b, a * W : a * W + ROWS, :], tap(w_ref, 3 * a + b))
    sig = jax.nn.sigmoid(spatial)
    hidden = (spatial * sig).astype(BF)
    hidden_ref[...] = hidden
    slope_ref[...] = sig * (1.0 + spatial * (1.0 - sig))
    grads = [
        dot_tn(hidden, other)
        for other in (cot_next[...], cot[...].astype(BF), cot_prev[...])
    ]
    pad = jnp.zeros((4, C), F32)
    for half in range(2):
        for y in range(4):
            both = []
            for core in range(2):
                r = half * HALF + y * PART + core * OWN
                both.append(jnp.concatenate([g[r : r + OWN, :] for g in grads] + [pad], axis=0))
            mine = jnp.where(c == 0, both[0], both[1])
            theirs = jnp.where(c == 0, both[1], both[0])
            for x in range(4):
                mine_ref[x, y, half] = mine[16 * x : 16 * x + 16, :]
                theirs_ref[x, y, half] = theirs[16 * x : 16 * x + 16, :]


def split_kernel(place, parts, keep_ref, give_ref):
    h = place[1]
    total = parts[0]
    for i in range(1, 16):
        total = total + parts[i]
    keep_ref[...] = jnp.where(h == 0, total[0], total[1])
    give_ref[...] = jnp.where(h == 0, total[1], total[0])


def backward_kernel(w_ref, slope, cot, cot_prev, cot_next, grad_ref, windows):
    gh = dot_nt(cot_next[...], tap(w_ref, 9))
    gh = gh + dot_nt(cot[...].astype(BF), tap(w_ref, 10))
    gh = gh + dot_nt(cot_prev[...], tap(w_ref, 11))
    gs = (gh * slope[...]).astype(BF).astype(F32)
    fill_windows(windows, gs)
    acc = cot[...]
    for a in range(3):
        for b in range(3):
            acc = acc + dot_nt(windows[2 - b, (2 - a) * W : (2 - a) * W + ROWS, :], tap(w_ref, 3 * a + b))
    grad_ref[...] = acc


def output_kernel(w_ref, video, hidden, prev, after, out_ref):
    acc = video[...] + dot(hidden[...], tap(w_ref, 10))
    acc = acc + dot(prev[...], tap(w_ref, 9))
    out_ref[...] = acc + dot(after[...], tap(w_ref, 11))


def kernel_call(body, outs, ins, scratch, micros, name):
    whole = pl.BlockSpec(memory_space=pltpu.VMEM)
    specs = [pl.BlockSpec(memory_space=pltpu.SMEM) if a.shape == (2,) else whole for a in ins]
    return pl.pallas_call(
        body,
        out_shape=tuple(jax.ShapeDtypeStruct(*o) for o in outs),
        in_specs=specs,
        out_specs=tuple(whole for _ in outs),
        scratch_shapes=scratch,
        compiler_params=pltpu.CompilerParams(vmem_limit_bytes=48 * 1024 * 1024),
        cost_estimate=pl.CostEstimate(flops=int(micros * 1.0e9), bytes_accessed=1_000_000, transcendentals=0),
        name=name,
    )(*ins)


def on_device(video, spatial_w, spatial_b, temporal_w, cotangent):
    tie = lax.optimization_barrier
    c, h, x = lax.axis_index("c"), lax.axis_index("h"), lax.axis_index("x")
    place = jnp.stack([c, h]).astype(jnp.int32)
    shape = video.shape
    video_f = video.reshape(ROWS, C)
    cot_f = cotangent.reshape(ROWS, C)
    cot_b = cot_f.astype(BF)

    w = jnp.concatenate([spatial_w, temporal_w.astype(BF)], axis=0)
    other = across(lax.dynamic_slice_in_dim(w, 3 * x, 3, 0))
    own_m = lax.all_gather(w, "y")
    other, own_m, cot_b = tie((other, own_m, cot_b))
    oth_m = to_all(other, PLANE)
    own_t = core_swap(own_m)
    cot_next = lax.ppermute(cot_b, TM, FRAMES_DOWN)
    cot_prev = lax.ppermute(cot_b, TM, FRAMES_UP)
    own, windows = kernel_call(
        prepare_kernel,
        [((TAPS, 1, HALF, C), BF), ((3, ROWS + 2 * W, C), BF)],
        (place, own_m, own_t, video_f), [], 100, "prepare",
    )
    oth_m, own, windows = tie((oth_m, own, windows))
    oth_t = core_swap(oth_m)

    w_all, hidden, slope, mine, theirs = kernel_call(
        forward_kernel,
        [
            ((TAPS, 2, HALF, C), BF), ((ROWS, C), BF), ((ROWS, C), F32),
            ((4, 4, 2, 16, C), F32), ((4, 4, 2, 16, C), F32),
        ],
        (place, own, oth_m, oth_t, windows, spatial_b.reshape(1, C), cot_f, cot_prev, cot_next),
        [], 6, "forward",
    )

    part = mine + core_swap(theirs)
    part = lax.all_to_all(part.reshape(16, 2, 16, C), PLANE, 0, 0, tiled=True)
    prev = lax.ppermute(hidden, TM, FRAMES_UP)
    after = lax.ppermute(hidden, TM, FRAMES_DOWN)
    keep, give = kernel_call(
        split_kernel, [((16, C), F32), ((16, C), F32)], (place, part), [], 100, "split",
    )
    part = keep + across(give)
    part, slope = tie((part, slope))
    part = to_all(part, Z_LO)
    (grad_video,) = kernel_call(
        backward_kernel, [((ROWS, C), F32)], (w_all, slope, cot_f, cot_prev, cot_next),
        [pltpu.VMEM((3, ROWS + 2 * W, C), BF)], 5, "backward",
    )
    part, grad_video = tie((part, grad_video))
    part = jnp.sum(part, axis=0)
    part, video_f = tie((part, video_f))
    part = to_all(part, "x").reshape(4 * 16, C)
    (output,) = kernel_call(
        output_kernel, [((ROWS, C), F32)], (w_all, video_f, hidden, prev, after), [], 3, "output",
    )
    total_rows = ROWS * lax.axis_size(TM) * lax.axis_size(CLIP)
    grad_temporal = part[: 3 * OWN].reshape(3, OWN, C) * (1.0 / math.sqrt(total_rows))
    return output.reshape(shape), grad_video.reshape(shape), grad_temporal


def solution(mesh):
    finer = Mesh(mesh.devices.reshape(SIZES), AXES)
    placed = (
        P(CLIP, TM, None, None, None),
        P(None, CLIP, None),
        P(),
        P(None, CLIP, None),
        P(CLIP, TM, None, None, None),
    )
    return jax.shard_map(
        on_device,
        mesh=finer,
        in_specs=placed,
        out_specs=(
            P(CLIP, TM, None, None, None),
            P(CLIP, TM, None, None, None),
            P(None, CLIP, None),
        ),
        check_vma=False,
    )
```

```python
import math

import jax
import jax.numpy as jnp
from jax import lax
from jax.experimental import pallas as pl
from jax.experimental.pallas import tpu as pltpu
from jax.sharding import Mesh
from jax.sharding import PartitionSpec as P

AXES = ("x", "m", "k", "h", "y", "c")
SIZES = (4, 2, 4, 2, 4, 2)
TM = ("x", "m", "k")
Z_LO = ("m", "k")
CLIP = ("h", "y", "c")
PLANE = ("x", "y")
H, W, C = 16, 32, 320
ROWS = H * W
HALF, PART, OWN = 160, 40, 20
TAPS = 12
BF = jnp.bfloat16
F32 = jnp.float32


def pairs_across():
    def place(z):
        return (z % 8) * 2 + z // 8

    there = [(z - 4) % 16 if z % 8 < 4 else (z + 4) % 16 for z in range(16)]
    return [(place(z), place(there[z])) for z in range(16)]


ACROSS = pairs_across()
FRAMES_UP = [(t, t + 1) for t in range(31) if t % 8 != 7]
FRAMES_DOWN = [(u, t) for t, u in FRAMES_UP]
FRAMES_FAR = [p for t in (7, 15, 23) for p in ((t, t + 1), (t + 1, t))]


def across(a):
    return lax.ppermute(a, ("m", "k", "h"), ACROSS)


def core_swap(a):
    return lax.ppermute(a, "c", [(0, 1), (1, 0)])


def to_all(a, axes):
    n = lax.axis_size(axes)
    return lax.all_to_all(jnp.broadcast_to(a[None], (n, *a.shape)), axes, 0, 0, tiled=True)


def dot(a, b):
    return lax.dot_general(a, b, (((1,), (0,)), ((), ())), preferred_element_type=F32)


def dot_nt(a, b):
    return lax.dot_general(a, b, (((1,), (1,)), ((), ())), preferred_element_type=F32)


def dot_tn(a, b):
    return lax.dot_general(a, b, (((0,), (0,)), ((), ())), preferred_element_type=F32)


def fill_windows(windows, value):
    col = lax.broadcasted_iota(jnp.int32, (ROWS, 1), 0) % W
    edge = jnp.zeros((W, C), BF)
    for d in range(3):
        windows[d, 0:W, :] = edge
        windows[d, W + ROWS : 2 * W + ROWS, :] = edge
    windows[1, W : W + ROWS, :] = value.astype(BF)
    left = jnp.where(col == 0, 0.0, pltpu.roll(value, 1, 0))
    windows[0, W : W + ROWS, :] = left.astype(BF)
    right = jnp.where(col == W - 1, 0.0, pltpu.roll(value, ROWS - 1, 0))
    windows[2, W : W + ROWS, :] = right.astype(BF)


def tap(w_ref, t):
    return w_ref[t].reshape(C, C)


def join(w_ref, t, half, y, mine, theirs, c):
    low = jnp.where(c == 0, mine, theirs)
    high = jnp.where(c == 0, theirs, mine)
    w_ref[t, half, y * PART : (y + 1) * PART, :] = jnp.concatenate([low, high], axis=0)


def sides(place, before, after, far):
    first, last = place[2] == 0, place[2] == 7
    return jnp.where(first, far, before), jnp.where(last, far, after)


def conv(windows, w_ref, bias):
    acc = jnp.zeros((ROWS, C), F32) + bias
    for a in range(3):
        for b in range(3):
            acc = acc + dot(windows[b, a * W : a * W + ROWS, :], tap(w_ref, 3 * a + b))
    return acc


def prepare_kernel(place, own_m, own_t, video, w_ref, windows):
    c = place[0]
    for t in range(TAPS):
        for y in range(4):
            join(w_ref, t, 0, y, own_m[y, t], own_t[y, t], c)
    fill_windows(windows, video[...])


def forward_kernel(
    place, own, oth_m, oth_t, windows, bias, cot, cot_prev, cot_next, far,
    w_ref, hidden_ref, slope_ref, mine_ref, theirs_ref,
):
    c, h = place[0], place[1]
    for t in range(TAPS):
        w_ref[t, h] = own[t, 0]
        for y in range(4):
            source = (t // 3) * 4 + y
            join(w_ref, t, 1 - h, y, oth_m[source, t % 3], oth_t[source, t % 3], c)
    spatial = conv(windows, w_ref, bias[...])
    sig = jax.nn.sigmoid(spatial)
    hidden = (spatial * sig).astype(BF)
    hidden_ref[...] = hidden
    slope_ref[...] = sig * (1.0 + spatial * (1.0 - sig))
    before, after = sides(place, cot_prev[...], cot_next[...], far[0])
    grads = [dot_tn(hidden, other) for other in (after, cot[...].astype(BF), before)]
    pad = jnp.zeros((4, C), F32)
    for half in range(2):
        for y in range(4):
            both = []
            for core in range(2):
                r = half * HALF + y * PART + core * OWN
                both.append(jnp.concatenate([g[r : r + OWN, :] for g in grads] + [pad], axis=0))
            mine = jnp.where(c == 0, both[0], both[1])
            theirs = jnp.where(c == 0, both[1], both[0])
            for x in range(4):
                mine_ref[x, y, half] = mine[16 * x : 16 * x + 16, :]
                theirs_ref[x, y, half] = theirs[16 * x : 16 * x + 16, :]


def split_kernel(place, parts, keep_ref, give_ref):
    h = place[1]
    total = parts[0]
    for i in range(1, 16):
        total = total + parts[i]
    keep_ref[...] = jnp.where(h == 0, total[0], total[1])
    give_ref[...] = jnp.where(h == 0, total[1], total[0])


def backward_kernel(place, w_ref, slope, cot, cot_prev, cot_next, far, grad_ref, windows):
    before, after = sides(place, cot_prev[...], cot_next[...], far[0])
    gh = dot_nt(after, tap(w_ref, 9))
    gh = gh + dot_nt(cot[...].astype(BF), tap(w_ref, 10))
    gh = gh + dot_nt(before, tap(w_ref, 11))
    gs = (gh * slope[...]).astype(BF).astype(F32)
    fill_windows(windows, gs)
    acc = cot[...]
    for a in range(3):
        for b in range(3):
            acc = acc + dot_nt(windows[2 - b, (2 - a) * W : (2 - a) * W + ROWS, :], tap(w_ref, 3 * a + b))
    grad_ref[...] = acc


def far_kernel(place, w_ref, far, bias, hidden_ref, windows):
    fill_windows(windows, far[1].astype(F32))
    spatial = conv(windows, w_ref, bias[...])
    hidden = (spatial * jax.nn.sigmoid(spatial)).astype(BF)
    hidden_ref[...] = jnp.where(place[3] == 1, hidden, jnp.zeros_like(hidden))


def output_kernel(place, w_ref, video, hidden, prev, after, far, out_ref):
    before, behind = sides(place, prev[...], after[...], far[...])
    acc = video[...] + dot(hidden[...], tap(w_ref, 10))
    acc = acc + dot(before, tap(w_ref, 9))
    out_ref[...] = acc + dot(behind, tap(w_ref, 11))


def kernel_call(body, outs, ins, scratch, micros, name):
    whole = pl.BlockSpec(memory_space=pltpu.VMEM)
    specs = [pl.BlockSpec(memory_space=pltpu.SMEM) if a.shape == (4,) else whole for a in ins]
    return pl.pallas_call(
        body,
        out_shape=tuple(jax.ShapeDtypeStruct(*o) for o in outs),
        in_specs=specs,
        out_specs=tuple(whole for _ in outs),
        scratch_shapes=scratch,
        compiler_params=pltpu.CompilerParams(vmem_limit_bytes=48 * 1024 * 1024),
        cost_estimate=pl.CostEstimate(flops=int(micros * 1.0e9), bytes_accessed=1_000_000, transcendentals=0),
        name=name,
    )(*ins)


def on_device(video, spatial_w, spatial_b, temporal_w, cotangent):
    tie = lax.optimization_barrier
    c, h, x, z = (lax.axis_index(a) for a in ("c", "h", "x", Z_LO))
    wrapped = ((z == 0) & (x > 0)) | ((z == 7) & (x < 3))
    place = jnp.stack([c, h, z, wrapped.astype(jnp.int32)]).astype(jnp.int32)
    shape = video.shape
    video_f = video.reshape(ROWS, C)
    cot_f = cotangent.reshape(ROWS, C)
    bias = spatial_b.reshape(1, C)

    both = jnp.stack([cot_f, video_f]).astype(BF)
    cot_b = both[0]
    far = lax.ppermute(both, TM, FRAMES_FAR)
    w = jnp.concatenate([spatial_w, temporal_w.astype(BF)], axis=0)
    other = across(lax.dynamic_slice_in_dim(w, 3 * x, 3, 0))
    own_m = lax.all_gather(w, "y")
    cot_next = lax.ppermute(cot_b, TM, FRAMES_DOWN)
    cot_prev = lax.ppermute(cot_b, TM, FRAMES_UP)
    other, own_m, cot_next, cot_prev = tie((other, own_m, cot_next, cot_prev))
    oth_m = to_all(other, PLANE)
    own_t = core_swap(own_m)
    own, windows = kernel_call(
        prepare_kernel,
        [((TAPS, 1, HALF, C), BF), ((3, ROWS + 2 * W, C), BF)],
        (place, own_m, own_t, video_f), [], 0.01, "prepare",
    )
    oth_m, own, windows, far = tie((oth_m, own, windows, far))
    oth_t = core_swap(oth_m)

    w_all, hidden, slope, mine, theirs = kernel_call(
        forward_kernel,
        [
            ((TAPS, 2, HALF, C), BF), ((ROWS, C), BF), ((ROWS, C), F32),
            ((4, 4, 2, 16, C), F32), ((4, 4, 2, 16, C), F32),
        ],
        (place, own, oth_m, oth_t, windows, bias, cot_f, cot_prev, cot_next, far),
        [], 6, "forward",
    )

    part = mine + core_swap(theirs)
    part = lax.all_to_all(part.reshape(16, 2, 16, C), PLANE, 0, 0, tiled=True)
    prev = lax.ppermute(hidden, TM, FRAMES_UP)
    after = lax.ppermute(hidden, TM, FRAMES_DOWN)
    (hidden_far,) = kernel_call(
        far_kernel, [((ROWS, C), BF)], (place, w_all, far, bias),
        [pltpu.VMEM((3, ROWS + 2 * W, C), BF)], 5, "far",
    )
    part, prev, after, hidden_far = tie((part, prev, after, hidden_far))
    keep, give = kernel_call(
        split_kernel, [((16, C), F32), ((16, C), F32)], (place, part), [], 0.01, "split",
    )
    part = keep + across(give)
    part, slope = tie((part, slope))
    part = to_all(part, Z_LO)
    (grad_video,) = kernel_call(
        backward_kernel, [((ROWS, C), F32)], (place, w_all, slope, cot_f, cot_prev, cot_next, far),
        [pltpu.VMEM((3, ROWS + 2 * W, C), BF)], 5, "backward",
    )
    part, grad_video = tie((part, grad_video))
    part = jnp.sum(part, axis=0)
    part, video_f = tie((part, video_f))
    part = to_all(part, "x").reshape(4 * 16, C)
    (output,) = kernel_call(
        output_kernel, [((ROWS, C), F32)], (place, w_all, video_f, hidden, prev, after, hidden_far), [], 3, "output",
    )
    total_rows = ROWS * lax.axis_size(TM) * lax.axis_size(CLIP)
    grad_temporal = part[: 3 * OWN].reshape(3, OWN, C) * (1.0 / math.sqrt(total_rows))
    return output.reshape(shape), grad_video.reshape(shape), grad_temporal


def solution(mesh):
    finer = Mesh(mesh.devices.reshape(SIZES), AXES)
    placed = (
        P(CLIP, TM, None, None, None),
        P(None, CLIP, None),
        P(),
        P(None, CLIP, None),
        P(CLIP, TM, None, None, None),
    )
    return jax.shard_map(
        on_device,
        mesh=finer,
        in_specs=placed,
        out_specs=(
            P(CLIP, TM, None, None, None),
            P(CLIP, TM, None, None, None),
            P(None, CLIP, None),
        ),
        check_vma=False,
    )
```

```python
import math

import jax
import jax.numpy as jnp
from jax import lax
from jax.experimental import pallas as pl
from jax.experimental.pallas import tpu as pltpu
from jax.sharding import Mesh
from jax.sharding import PartitionSpec as P

AXES = ("x", "m", "k", "h", "y", "c")
SIZES = (4, 2, 4, 2, 4, 2)
TM = ("x", "m", "k")
Z_LO = ("m", "k")
CLIP = ("h", "y", "c")
PLANE = ("x", "y")
H, W, C = 16, 32, 320
ROWS = H * W
HALF, PART, OWN = 160, 40, 20
TAPS = 12
SPACE = 9
WIDE = 384
SLOT = 64
BF = jnp.bfloat16
F32 = jnp.float32


def pairs_across():
    def place(z):
        return (z % 8) * 2 + z // 8

    there = [(z - 4) % 16 if z % 8 < 4 else (z + 4) % 16 for z in range(16)]
    return [(place(z), place(there[z])) for z in range(16)]


ACROSS = pairs_across()
FRAMES_UP = [(t, t + 1) for t in range(31) if t % 8 != 7]
FRAMES_DOWN = [(u, t) for t, u in FRAMES_UP]
FRAMES_FAR = [p for t in (7, 15, 23) for p in ((t, t + 1), (t + 1, t))]


def across(a):
    return lax.ppermute(a, ("m", "k", "h"), ACROSS)


def core_swap(a):
    return lax.ppermute(a, "c", [(0, 1), (1, 0)])


def to_all(a, axes):
    n = lax.axis_size(axes)
    return lax.all_to_all(jnp.broadcast_to(a[None], (n, *a.shape)), axes, 0, 0, tiled=True)


def dot(a, b):
    return lax.dot_general(a, b, (((1,), (0,)), ((), ())), preferred_element_type=F32)


def dot_nt(a, b):
    return lax.dot_general(a, b, (((1,), (1,)), ((), ())), preferred_element_type=F32)


def dot_tn(a, b):
    return lax.dot_general(a, b, (((0,), (0,)), ((), ())), preferred_element_type=F32)


def fill_windows(windows, value):
    col = lax.broadcasted_iota(jnp.int32, (ROWS, 1), 0) % W
    edge = jnp.zeros((W, C), BF)
    for d in range(3):
        windows[d, 0:W, :] = edge
        windows[d, W + ROWS : 2 * W + ROWS, :] = edge
    windows[1, W : W + ROWS, :] = value.astype(BF)
    left = jnp.where(col == 0, 0.0, pltpu.roll(value, 1, 0))
    windows[0, W : W + ROWS, :] = left.astype(BF)
    right = jnp.where(col == W - 1, 0.0, pltpu.roll(value, ROWS - 1, 0))
    windows[2, W : W + ROWS, :] = right.astype(BF)


def tap(w_ref, t):
    return w_ref[t].reshape(C, C)


def join(w_ref, t, half, y, mine, theirs, c):
    low = jnp.where(c == 0, mine, theirs)
    high = jnp.where(c == 0, theirs, mine)
    w_ref[t, half, y * PART : (y + 1) * PART, :] = jnp.concatenate([low, high], axis=0)


def sides(place, before, after, far):
    first, last = place[2] == 0, place[2] == 7
    return jnp.where(first, far, before), jnp.where(last, far, after)


def conv(windows, w_ref, bias):
    acc = jnp.zeros((ROWS, C), F32) + bias
    for a in range(3):
        for b in range(3):
            acc = acc + dot(windows[b, a * W : a * W + ROWS, :], tap(w_ref, 3 * a + b))
    return acc


def copies(sems, *pairs):
    started = [pltpu.make_async_copy(src, dst, sems.at[i]) for i, (src, dst) in enumerate(pairs)]
    for one in started:
        one.start()
    return started


def prepare_kernel(video, out, windows, sems):
    fill_windows(windows, video[...])
    for one in copies(sems, (windows, out)):
        one.wait()


def forward_kernel(
    place, w_mine_h, w_theirs_h, windows_h, bias, cot_h, prev_h, next_h, far_h,
    w_h, hidden_h, slope_h, mine_ref, theirs_ref,
    w_mine, w_theirs, windows, cot, cot_prev, cot_next, far, w_ref, hidden_ref, slope_ref, sems,
):
    c, h = place[0], place[1]
    arrive = copies(
        sems, (w_mine_h, w_mine), (w_theirs_h, w_theirs), (windows_h, windows),
        (cot_h, cot), (prev_h, cot_prev), (next_h, cot_next), (far_h, far),
    )
    leave = [
        pltpu.make_async_copy(src, dst, sems.at[7 + i])
        for i, (src, dst) in enumerate(((w_ref, w_h), (hidden_ref, hidden_h), (slope_ref, slope_h)))
    ]
    arrive[0].wait()
    arrive[1].wait()
    for t in range(TAPS):
        for y in range(4):
            source = (t // 3) * 4 + y
            for i, half in ((0, h), (1, 1 - h)):
                at = i * SLOT + (t % 3) * OWN
                join(w_ref, t, half, y, w_mine[source, at : at + OWN, 0:C], w_theirs[source, at : at + OWN, 0:C], c)
    leave[0].start()
    for one in arrive[2:]:
        one.wait()
    spatial = conv(windows, w_ref, bias[...])
    sig = jax.nn.sigmoid(spatial)
    hidden = (spatial * sig).astype(BF)
    hidden_ref[...] = hidden
    slope_ref[...] = sig * (1.0 + spatial * (1.0 - sig))
    leave[1].start()
    leave[2].start()
    before, after = sides(place, cot_prev[...], cot_next[...], far[...])
    grads = [dot_tn(hidden, other) for other in (after, cot[...].astype(BF), before)]
    pad = jnp.zeros((4, C), F32)
    for half in range(2):
        for y in range(4):
            both = []
            for core in range(2):
                r = half * HALF + y * PART + core * OWN
                both.append(jnp.concatenate([g[r : r + OWN, :] for g in grads] + [pad], axis=0))
            mine = jnp.where(c == 0, both[0], both[1])
            theirs = jnp.where(c == 0, both[1], both[0])
            for x in range(4):
                mine_ref[x, y, half] = mine[16 * x : 16 * x + 16, :]
                theirs_ref[x, y, half] = theirs[16 * x : 16 * x + 16, :]
    for one in leave:
        one.wait()


def split_kernel(place, parts, keep_ref, give_ref):
    h = place[1]
    total = parts[0]
    for i in range(1, 16):
        total = total + parts[i]
    keep_ref[...] = jnp.where(h == 0, total[0], total[1])
    give_ref[...] = jnp.where(h == 0, total[1], total[0])


def backward_kernel(
    place, w_h, slope_h, cot_h, prev_h, next_h, far_h, grad_ref,
    w_ref, slope, cot, cot_prev, cot_next, far, windows, sems,
):
    arrive = copies(
        sems, (w_h.at[SPACE:TAPS], w_ref.at[SPACE:TAPS]), (cot_h, cot), (prev_h, cot_prev), (next_h, cot_next),
        (far_h, far), (slope_h, slope), (w_h.at[0:SPACE], w_ref.at[0:SPACE]),
    )
    for one in arrive[:5]:
        one.wait()
    before, after = sides(place, cot_prev[...], cot_next[...], far[...])
    gh = dot_nt(after, tap(w_ref, 9))
    gh = gh + dot_nt(cot[...].astype(BF), tap(w_ref, 10))
    gh = gh + dot_nt(before, tap(w_ref, 11))
    arrive[5].wait()
    gs = (gh * slope[...]).astype(BF).astype(F32)
    fill_windows(windows, gs)
    arrive[6].wait()
    acc = cot[...]
    for a in range(3):
        for b in range(3):
            acc = acc + dot_nt(windows[2 - b, (2 - a) * W : (2 - a) * W + ROWS, :], tap(w_ref, 3 * a + b))
    grad_ref[...] = acc


def far_kernel(place, w_h, far_h, bias, hidden_h, w_ref, far, hidden_ref, windows, sems):
    arrive = copies(sems, (far_h, far), (w_h.at[0:SPACE], w_ref))
    arrive[0].wait()
    fill_windows(windows, far[...].astype(F32))
    arrive[1].wait()
    spatial = conv(windows, w_ref, bias[...])
    hidden = (spatial * jax.nn.sigmoid(spatial)).astype(BF)
    hidden_ref[...] = jnp.where(place[3] == 1, hidden, jnp.zeros_like(hidden))
    for one in copies(sems, (hidden_ref, hidden_h)):
        one.wait()


def output_kernel(
    place, w_h, video_h, hidden_h, prev_h, after_h, far_h, out_ref,
    w_ref, video, hidden, prev, after, far, sems,
):
    for one in copies(
        sems, (w_h.at[SPACE:TAPS], w_ref), (video_h, video), (hidden_h, hidden), (prev_h, prev), (after_h, after), (far_h, far),
    ):
        one.wait()
    before, behind = sides(place, prev[...], after[...], far[...])
    acc = video[...] + dot(hidden[...], tap(w_ref, 1))
    acc = acc + dot(before, tap(w_ref, 0))
    out_ref[...] = acc + dot(behind, tap(w_ref, 2))


FRAME_B = (ROWS, C), BF
FRAME_F = (ROWS, C), F32
WINDOWS = (3, ROWS + 2 * W, C), BF
WEIGHTS = (TAPS, 2, HALF, C), BF
PIECES = (16, 2 * SLOT, WIDE), BF
SUMS = (4, 4, 2, 16, C), F32
SHARE = (16, C), F32


def kernel_call(body, ins, outs, scratch, copied, micros, name):
    spaces = {"s": pltpu.SMEM, "v": pltpu.VMEM, "h": pltpu.HBM}
    specs = [[pl.BlockSpec(memory_space=spaces[o[-1]]) for o in group] for group in (ins, outs)]
    return pl.pallas_call(
        body,
        out_shape=tuple(jax.ShapeDtypeStruct(*o[0]) for o in outs),
        in_specs=specs[0],
        out_specs=tuple(specs[1]),
        scratch_shapes=[pltpu.VMEM(*o) for o in scratch] + [pltpu.SemaphoreType.DMA((copied,))] * (copied > 0),
        compiler_params=pltpu.CompilerParams(vmem_limit_bytes=(60 if copied else 8) * 1024 * 1024),
        cost_estimate=pl.CostEstimate(flops=int(micros * 1.0e9), bytes_accessed=1_000_000, transcendentals=0),
        name=name,
    )(*(a for a, _ in ins))


def on_device(video, spatial_w, spatial_b, temporal_w, cotangent):
    tie = lax.optimization_barrier
    c, h, x, z = (lax.axis_index(a) for a in ("c", "h", "x", Z_LO))
    wrapped = ((z == 0) & (x > 0)) | ((z == 7) & (x < 3))
    place = jnp.stack([c, h, z, wrapped.astype(jnp.int32)]).astype(jnp.int32)
    shape = video.shape
    video_f = video.reshape(ROWS, C)
    cot_f = cotangent.reshape(ROWS, C)
    bias = spatial_b.reshape(1, C)

    cot_b, video_b = cot_f.astype(BF), video_f.astype(BF)
    far = lax.ppermute(cot_b, TM, FRAMES_FAR)
    video_far = lax.ppermute(video_b, TM, FRAMES_FAR)
    w = jnp.concatenate([spatial_w, temporal_w.astype(BF)], axis=0)
    quarter = lax.dynamic_slice_in_dim(w, 3 * x, 3, 0).reshape(3 * OWN, C)
    quarter = jnp.pad(quarter, ((0, SLOT - 3 * OWN), (0, WIDE - C)))
    other = across(quarter)
    cot_next = lax.ppermute(cot_b, TM, FRAMES_DOWN)
    cot_prev = lax.ppermute(cot_b, TM, FRAMES_UP)
    other, cot_next, cot_prev = tie((other, cot_next, cot_prev))
    w_mine = to_all(jnp.concatenate([quarter, other], axis=0), PLANE)
    (windows,) = kernel_call(prepare_kernel, [(video_f, "v")], [(WINDOWS, "h")], [WINDOWS], 1, 0.01, "prepare")
    w_mine, windows, far, video_far = tie((w_mine, windows, far, video_far))
    w_theirs = core_swap(w_mine)

    w_all, hidden, slope, mine, theirs = kernel_call(
        forward_kernel,
        [
            (place, "s"), (w_mine, "h"), (w_theirs, "h"), (windows, "h"), (bias, "v"),
            (cot_f, "h"), (cot_prev, "h"), (cot_next, "h"), (far, "h"),
        ],
        [(WEIGHTS, "h"), (FRAME_B, "h"), (FRAME_F, "h"), (SUMS, "v"), (SUMS, "v")],
        [PIECES, PIECES, WINDOWS, FRAME_F, FRAME_B, FRAME_B, FRAME_B, WEIGHTS, FRAME_B, FRAME_F],
        10, 6, "forward",
    )

    part = mine + core_swap(theirs)
    part = lax.all_to_all(part.reshape(16, 2, 16, C), PLANE, 0, 0, tiled=True)
    prev = lax.ppermute(hidden, TM, FRAMES_UP)
    after = lax.ppermute(hidden, TM, FRAMES_DOWN)
    (hidden_far,) = kernel_call(
        far_kernel, [(place, "s"), (w_all, "h"), (video_far, "h"), (bias, "v")], [(FRAME_B, "h")],
        [((SPACE, 2, HALF, C), BF), FRAME_B, FRAME_B, WINDOWS], 2, 5, "far",
    )
    part, prev, after, hidden_far = tie((part, prev, after, hidden_far))
    keep, give = kernel_call(
        split_kernel, [(place, "s"), (part, "v")], [(SHARE, "v"), (SHARE, "v")], [], 0, 0.01, "split",
    )
    part = keep + across(give)
    part, slope = tie((part, slope))
    part = to_all(part, Z_LO)
    (grad_video,) = kernel_call(
        backward_kernel,
        [(place, "s"), (w_all, "h"), (slope, "h"), (cot_f, "h"), (cot_prev, "h"), (cot_next, "h"), (far, "h")],
        [(FRAME_F, "v")],
        [WEIGHTS, FRAME_F, FRAME_F, FRAME_B, FRAME_B, FRAME_B, WINDOWS], 7, 5, "backward",
    )
    part, grad_video = tie((part, grad_video))
    part = jnp.sum(part, axis=0)
    part, video_f = tie((part, video_f))
    part = to_all(part, "x").reshape(4 * 16, C)
    (output,) = kernel_call(
        output_kernel,
        [(place, "s"), (w_all, "h"), (video_f, "h"), (hidden, "h"), (prev, "h"), (after, "h"), (hidden_far, "h")],
        [(FRAME_F, "v")],
        [((3, 2, HALF, C), BF), FRAME_F, FRAME_B, FRAME_B, FRAME_B, FRAME_B], 6, 3, "output",
    )
    total_rows = ROWS * lax.axis_size(TM) * lax.axis_size(CLIP)
    grad_temporal = part[: 3 * OWN].reshape(3, OWN, C) * (1.0 / math.sqrt(total_rows))
    return output.reshape(shape), grad_video.reshape(shape), grad_temporal


def solution(mesh):
    finer = Mesh(mesh.devices.reshape(SIZES), AXES)
    placed = (
        P(CLIP, TM, None, None, None),
        P(None, CLIP, None),
        P(),
        P(None, CLIP, None),
        P(CLIP, TM, None, None, None),
    )
    return jax.shard_map(
        on_device,
        mesh=finer,
        in_specs=placed,
        out_specs=(
            P(CLIP, TM, None, None, None),
            P(CLIP, TM, None, None, None),
            P(None, CLIP, None),
        ),
        check_vma=False,
    )
```

```python
import math

import jax
import jax.numpy as jnp
from jax import lax
from jax.experimental import pallas as pl
from jax.experimental.pallas import tpu as pltpu
from jax.sharding import Mesh
from jax.sharding import PartitionSpec as P

AXES = ("x", "m", "k", "h", "y", "c")
SIZES = (4, 2, 4, 2, 4, 2)
TM = ("x", "m", "k")
Z_LO = ("m", "k")
CLIP = ("h", "y", "c")
PLANE = ("x", "y")
H, W, C = 16, 32, 320
ROWS = H * W
HALF, PART, OWN = 160, 40, 20
TAPS = 12
SPACE = 9
WIDE = 384
LIMIT = 48
SLOT = 64
BF = jnp.bfloat16
F32 = jnp.float32


def pairs_across():
    def place(z):
        return (z % 8) * 2 + z // 8

    there = [(z - 4) % 16 if z % 8 < 4 else (z + 4) % 16 for z in range(16)]
    return [(place(z), place(there[z])) for z in range(16)]


ACROSS = pairs_across()
FRAMES_UP = [(t, t + 1) for t in range(31) if t % 8 != 7]
FRAMES_DOWN = [(u, t) for t, u in FRAMES_UP]
FRAMES_FAR = [p for t in (7, 15, 23) for p in ((t, t + 1), (t + 1, t))]


def across(a):
    return lax.ppermute(a, ("m", "k", "h"), ACROSS)


def core_swap(a):
    return lax.ppermute(a, "c", [(0, 1), (1, 0)])


def to_all(a, axes):
    n = lax.axis_size(axes)
    return lax.all_to_all(jnp.broadcast_to(a[None], (n, *a.shape)), axes, 0, 0, tiled=True)


def dot(a, b):
    return lax.dot_general(a, b, (((1,), (0,)), ((), ())), preferred_element_type=F32)


def dot_nt(a, b):
    return lax.dot_general(a, b, (((1,), (1,)), ((), ())), preferred_element_type=F32)


def dot_tn(a, b):
    return lax.dot_general(a, b, (((0,), (0,)), ((), ())), preferred_element_type=F32)


def fill_windows(windows, value):
    col = lax.broadcasted_iota(jnp.int32, (ROWS, 1), 0) % W
    edge = jnp.zeros((W, C), BF)
    for d in range(3):
        windows[d, 0:W, :] = edge
        windows[d, W + ROWS : 2 * W + ROWS, :] = edge
    windows[1, W : W + ROWS, :] = value.astype(BF)
    left = jnp.where(col == 0, 0.0, pltpu.roll(value, 1, 0))
    windows[0, W : W + ROWS, :] = left.astype(BF)
    right = jnp.where(col == W - 1, 0.0, pltpu.roll(value, ROWS - 1, 0))
    windows[2, W : W + ROWS, :] = right.astype(BF)


def tap(w_ref, t):
    return w_ref[t].reshape(C, C)


def join(w_ref, t, half, y, mine, theirs, c):
    low = jnp.where(c == 0, mine, theirs)
    high = jnp.where(c == 0, theirs, mine)
    w_ref[t, half, y * PART : (y + 1) * PART, :] = jnp.concatenate([low, high], axis=0)


def sides(place, before, after, far):
    first, last = place[2] == 0, place[2] == 7
    return jnp.where(first, far, before), jnp.where(last, far, after)


def conv(windows, w_ref, bias):
    acc = jnp.zeros((ROWS, C), F32) + bias
    for a in range(3):
        for b in range(3):
            acc = acc + dot(windows[b, a * W : a * W + ROWS, :], tap(w_ref, 3 * a + b))
    return acc


def copies(sems, *pairs):
    started = [pltpu.make_async_copy(src, dst, sems.at[i]) for i, (src, dst) in enumerate(pairs)]
    for one in started:
        one.start()
    return started


def prepare_kernel(video, out, windows, sems):
    fill_windows(windows, video[...])
    for one in copies(sems, (windows, out)):
        one.wait()


def forward_kernel(
    place, own_m, own_t, oth_m, oth_t, windows, bias, cot, cot_prev, cot_next, far,
    w_h, hidden_ref, slope_ref, mine_ref, theirs_ref, w_ref, sems,
):
    c, h = place[0], place[1]
    for t in range(TAPS):
        for y in range(4):
            at = t * OWN
            join(w_ref, t, h, y, own_m[y, at : at + OWN, 0:C], own_t[y, at : at + OWN, 0:C], c)
            x, at = t // 3, y * SLOT + (t % 3) * OWN
            join(w_ref, t, 1 - h, y, oth_m[x, at : at + OWN, 0:C], oth_t[x, at : at + OWN, 0:C], c)
    leave = copies(sems, (w_ref, w_h))
    spatial = conv(windows, w_ref, bias[...])
    sig = jax.nn.sigmoid(spatial)
    hidden = (spatial * sig).astype(BF)
    hidden_ref[...] = hidden
    slope_ref[...] = sig * (1.0 + spatial * (1.0 - sig))
    before, after = sides(place, cot_prev[...], cot_next[...], far[...])
    grads = [dot_tn(hidden, other) for other in (after, cot[...].astype(BF), before)]
    pad = jnp.zeros((4, C), F32)
    for half in range(2):
        for y in range(4):
            both = []
            for core in range(2):
                r = half * HALF + y * PART + core * OWN
                both.append(jnp.concatenate([g[r : r + OWN, :] for g in grads] + [pad], axis=0))
            mine = jnp.where(c == 0, both[0], both[1])
            theirs = jnp.where(c == 0, both[1], both[0])
            for x in range(4):
                mine_ref[x, y, half] = mine[16 * x : 16 * x + 16, :]
                theirs_ref[x, y, half] = theirs[16 * x : 16 * x + 16, :]
    for one in leave:
        one.wait()


def split_kernel(place, parts, keep_ref, give_ref):
    h = place[1]
    total = parts[0]
    for i in range(1, 16):
        total = total + parts[i]
    keep_ref[...] = jnp.where(h == 0, total[0], total[1])
    give_ref[...] = jnp.where(h == 0, total[1], total[0])


def backward_kernel(
    place, w_h, slope_h, cot_h, prev_h, next_h, far_h, grad_ref,
    w_ref, slope, cot, cot_prev, cot_next, far, windows, sems,
):
    arrive = copies(
        sems, (w_h.at[SPACE:TAPS], w_ref.at[SPACE:TAPS]), (cot_h, cot), (prev_h, cot_prev), (next_h, cot_next),
        (far_h, far), (slope_h, slope), (w_h.at[0:SPACE], w_ref.at[0:SPACE]),
    )
    for one in arrive[:5]:
        one.wait()
    before, after = sides(place, cot_prev[...], cot_next[...], far[...])
    gh = dot_nt(after, tap(w_ref, 9))
    gh = gh + dot_nt(cot[...].astype(BF), tap(w_ref, 10))
    gh = gh + dot_nt(before, tap(w_ref, 11))
    arrive[5].wait()
    gs = (gh * slope[...]).astype(BF).astype(F32)
    fill_windows(windows, gs)
    arrive[6].wait()
    acc = cot[...]
    for a in range(3):
        for b in range(3):
            acc = acc + dot_nt(windows[2 - b, (2 - a) * W : (2 - a) * W + ROWS, :], tap(w_ref, 3 * a + b))
    grad_ref[...] = acc


def output_kernel(
    place, w_h, video_h, hidden_h, prev_h, after_h, far_h, out_ref,
    w_ref, video, hidden, prev, after, far, sems,
):
    for one in copies(
        sems, (w_h.at[SPACE:TAPS], w_ref), (video_h, video), (hidden_h, hidden), (prev_h, prev), (after_h, after), (far_h, far),
    ):
        one.wait()
    before, behind = sides(place, prev[...], after[...], far[...])
    acc = video[...] + dot(hidden[...], tap(w_ref, 1))
    acc = acc + dot(before, tap(w_ref, 0))
    out_ref[...] = acc + dot(behind, tap(w_ref, 2))


FRAME_B = (ROWS, C), BF
FRAME_F = (ROWS, C), F32
WINDOWS = (3, ROWS + 2 * W, C), BF
WEIGHTS = (TAPS, 2, HALF, C), BF
SUMS = (4, 4, 2, 16, C), F32
SHARE = (16, C), F32


def kernel_call(body, ins, outs, scratch, copied, micros, name, limit=60):
    spaces = {"s": pltpu.SMEM, "v": pltpu.VMEM, "h": pltpu.HBM}
    specs = [[pl.BlockSpec(memory_space=spaces[o[-1]]) for o in group] for group in (ins, outs)]
    return pl.pallas_call(
        body,
        out_shape=tuple(jax.ShapeDtypeStruct(*o[0]) for o in outs),
        in_specs=specs[0],
        out_specs=tuple(specs[1]),
        scratch_shapes=[pltpu.VMEM(*o) for o in scratch] + [pltpu.SemaphoreType.DMA((copied,))] * (copied > 0),
        compiler_params=pltpu.CompilerParams(vmem_limit_bytes=limit * 1024 * 1024),
        cost_estimate=pl.CostEstimate(flops=int(micros * 1.0e9), bytes_accessed=1_000_000, transcendentals=0),
        name=name,
    )(*(a for a, _ in ins))


def on_device(video, spatial_w, spatial_b, temporal_w, cotangent):
    tie = lax.optimization_barrier
    c, h, x, z = (lax.axis_index(a) for a in ("c", "h", "x", Z_LO))
    wrapped = ((z == 0) & (x > 0)) | ((z == 7) & (x < 3))
    place = jnp.stack([c, h, z, wrapped.astype(jnp.int32)]).astype(jnp.int32)
    shape = video.shape
    video_f = video.reshape(ROWS, C)
    cot_f = cotangent.reshape(ROWS, C)
    bias = spatial_b.reshape(1, C)

    cot_b = cot_f.astype(BF)
    w = jnp.concatenate([spatial_w, temporal_w.astype(BF)], axis=0)
    quarter = lax.dynamic_slice_in_dim(w, 3 * x, 3, 0).reshape(3 * OWN, C)
    other = across(jnp.pad(quarter, ((0, SLOT - 3 * OWN), (0, WIDE - C))))
    w = jnp.pad(w.reshape(TAPS * OWN, C), ((0, 0), (0, WIDE - C)))
    other, cot_b, w = tie((other, cot_b, w))
    cot_next = lax.ppermute(cot_b, TM, FRAMES_DOWN)
    cot_prev = lax.ppermute(cot_b, TM, FRAMES_UP)
    far = lax.ppermute(cot_b, TM, FRAMES_FAR)
    own_m = lax.all_gather(jnp.concatenate([w, other], axis=0), "y")
    oth_m = own_m[:, TAPS * OWN :].reshape(4 * SLOT, WIDE)
    oth_m, cot_next, cot_prev, far = tie((oth_m, cot_next, cot_prev, far))
    oth_m = lax.all_gather(oth_m, "x")
    (windows,) = kernel_call(prepare_kernel, [(video_f, "v")], [(WINDOWS, "h")], [WINDOWS], 1, 0.01, "prepare")
    oth_m, own_m, windows = tie((oth_m, own_m, windows))
    own_t, oth_t = core_swap(own_m), core_swap(oth_m)

    w_all, hidden, slope, mine, theirs = kernel_call(
        forward_kernel,
        [
            (place, "s"), (own_m, "v"), (own_t, "v"), (oth_m, "v"), (oth_t, "v"), (windows, "v"), (bias, "v"),
            (cot_f, "v"), (cot_prev, "v"), (cot_next, "v"), (far, "v"),
        ],
        [(WEIGHTS, "h"), (FRAME_B, "v"), (FRAME_F, "v"), (SUMS, "v"), (SUMS, "v")],
        [WEIGHTS], 1, 0.01, "forward", LIMIT,
    )
    part = mine + core_swap(theirs)
    part = lax.all_to_all(part.reshape(16, 2, 16, C), PLANE, 0, 0, tiled=True)
    prev = lax.ppermute(hidden, TM, FRAMES_UP)
    after = lax.ppermute(hidden, TM, FRAMES_DOWN)
    hidden_far = lax.ppermute(hidden, TM, FRAMES_FAR)
    keep, give = kernel_call(
        split_kernel, [(place, "s"), (part, "v")], [(SHARE, "v"), (SHARE, "v")], [], 0, 1000, "split", 8,
    )
    part = keep + across(give)
    part, slope, prev, after, hidden_far = tie((part, slope, prev, after, hidden_far))
    part = to_all(part, Z_LO)
    (grad_video,) = kernel_call(
        backward_kernel,
        [(place, "s"), (w_all, "h"), (slope, "h"), (cot_f, "h"), (cot_prev, "h"), (cot_next, "h"), (far, "h")],
        [(FRAME_F, "v")],
        [WEIGHTS, FRAME_F, FRAME_F, FRAME_B, FRAME_B, FRAME_B, WINDOWS], 7, 5, "backward",
    )
    part, grad_video = tie((part, grad_video))
    part = jnp.sum(part, axis=0)
    part, video_f = tie((part, video_f))
    part = to_all(part, "x").reshape(4 * 16, C)
    (output,) = kernel_call(
        output_kernel,
        [(place, "s"), (w_all, "h"), (video_f, "h"), (hidden, "h"), (prev, "h"), (after, "h"), (hidden_far, "h")],
        [(FRAME_F, "v")],
        [((3, 2, HALF, C), BF), FRAME_F, FRAME_B, FRAME_B, FRAME_B, FRAME_B], 6, 3, "output",
    )
    total_rows = ROWS * lax.axis_size(TM) * lax.axis_size(CLIP)
    grad_temporal = part[: 3 * OWN].reshape(3, OWN, C) * (1.0 / math.sqrt(total_rows))
    return output.reshape(shape), grad_video.reshape(shape), grad_temporal


def solution(mesh):
    finer = Mesh(mesh.devices.reshape(SIZES), AXES)
    placed = (
        P(CLIP, TM, None, None, None),
        P(None, CLIP, None),
        P(),
        P(None, CLIP, None),
        P(CLIP, TM, None, None, None),
    )
    return jax.shard_map(
        on_device,
        mesh=finer,
        in_specs=placed,
        out_specs=(
            P(CLIP, TM, None, None, None),
            P(CLIP, TM, None, None, None),
            P(None, CLIP, None),
        ),
        check_vma=False,
    )
```

```python
import math

import jax
import jax.numpy as jnp
from jax import lax
from jax.experimental import pallas as pl
from jax.experimental.pallas import tpu as pltpu
from jax.sharding import Mesh
from jax.sharding import PartitionSpec as P

AXES = ("x", "m", "k", "h", "y", "c")
SIZES = (4, 2, 4, 2, 4, 2)
TM = ("x", "m", "k")
Z_LO = ("m", "k")
CLIP = ("h", "y", "c")
PLANE = ("x", "y")
H, W, C = 16, 32, 320
ROWS = H * W
HALF, PART, OWN = 160, 40, 20
TAPS = 12
SPACE = 9
WIDE = 384
LIMIT = 48
SLOT = 64
BF = jnp.bfloat16
F32 = jnp.float32


def pairs_across():
    def place(z):
        return (z % 8) * 2 + z // 8

    there = [(z - 4) % 16 if z % 8 < 4 else (z + 4) % 16 for z in range(16)]
    return [(place(z), place(there[z])) for z in range(16)]


ACROSS = pairs_across()
FRAMES_UP = [(t, t + 1) for t in range(31) if t % 8 != 7]
FRAMES_DOWN = [(u, t) for t, u in FRAMES_UP]
FRAMES_FAR = [p for t in (7, 15, 23) for p in ((t, t + 1), (t + 1, t))]


def across(a):
    return lax.ppermute(a, ("m", "k", "h"), ACROSS)


def core_swap(a):
    return lax.ppermute(a, "c", [(0, 1), (1, 0)])


def to_all(a, axes):
    n = lax.axis_size(axes)
    return lax.all_to_all(jnp.broadcast_to(a[None], (n, *a.shape)), axes, 0, 0, tiled=True)


def dot(a, b):
    return lax.dot_general(a, b, (((1,), (0,)), ((), ())), preferred_element_type=F32)


def dot_nt(a, b):
    return lax.dot_general(a, b, (((1,), (1,)), ((), ())), preferred_element_type=F32)


def dot_tn(a, b):
    return lax.dot_general(a, b, (((0,), (0,)), ((), ())), preferred_element_type=F32)


def fill_windows(windows, value):
    col = lax.broadcasted_iota(jnp.int32, (ROWS, 1), 0) % W
    edge = jnp.zeros((W, C), BF)
    for d in range(3):
        windows[d, 0:W, :] = edge
        windows[d, W + ROWS : 2 * W + ROWS, :] = edge
    windows[1, W : W + ROWS, :] = value.astype(BF)
    left = jnp.where(col == 0, 0.0, pltpu.roll(value, 1, 0))
    windows[0, W : W + ROWS, :] = left.astype(BF)
    right = jnp.where(col == W - 1, 0.0, pltpu.roll(value, ROWS - 1, 0))
    windows[2, W : W + ROWS, :] = right.astype(BF)


def tap(w_ref, t):
    return w_ref[t].reshape(C, C)


def join(w_ref, t, half, y, mine, theirs, c):
    low = jnp.where(c == 0, mine, theirs)
    high = jnp.where(c == 0, theirs, mine)
    w_ref[t, half, y * PART : (y + 1) * PART, :] = jnp.concatenate([low, high], axis=0)


def sides(place, before, after, far):
    first, last = place[2] == 0, place[2] == 7
    return jnp.where(first, far, before), jnp.where(last, far, after)


def conv(windows, w_ref, bias):
    acc = jnp.zeros((ROWS, C), F32) + bias
    for a in range(3):
        for b in range(3):
            acc = acc + dot(windows[b, a * W : a * W + ROWS, :], tap(w_ref, 3 * a + b))
    return acc


def copies(sems, *pairs):
    started = [pltpu.make_async_copy(src, dst, sems.at[i]) for i, (src, dst) in enumerate(pairs)]
    for one in started:
        one.start()
    return started


def prepare_kernel(video, windows):
    fill_windows(windows, video[...])


def apart_kernel(gathered, out):
    for y in range(4):
        out[y * SLOT : (y + 1) * SLOT, :] = gathered[y, TAPS * OWN : TAPS * OWN + SLOT, :]


def forward_kernel(
    place, own_m, own_t, oth_m, oth_t, windows, bias, cot, cot_prev, cot_next, far,
    w_h, hidden_ref, slope_ref, mine_ref, theirs_ref, w_ref, sems,
):
    c, h = place[0], place[1]
    for t in range(TAPS):
        for y in range(4):
            at = t * OWN
            join(w_ref, t, h, y, own_m[y, at : at + OWN, 0:C], own_t[y, at : at + OWN, 0:C], c)
            x, at = t // 3, y * SLOT + (t % 3) * OWN
            join(w_ref, t, 1 - h, y, oth_m[x, at : at + OWN, 0:C], oth_t[x, at : at + OWN, 0:C], c)
    leave = copies(sems, (w_ref, w_h))
    spatial = conv(windows, w_ref, bias[...])
    sig = jax.nn.sigmoid(spatial)
    hidden = (spatial * sig).astype(BF)
    hidden_ref[...] = hidden
    slope_ref[...] = sig * (1.0 + spatial * (1.0 - sig))
    before, after = sides(place, cot_prev[...], cot_next[...], far[...])
    grads = [dot_tn(hidden, other) for other in (after, cot[...].astype(BF), before)]
    pad = jnp.zeros((4, C), F32)
    for half in range(2):
        for y in range(4):
            both = []
            for core in range(2):
                r = half * HALF + y * PART + core * OWN
                both.append(jnp.concatenate([g[r : r + OWN, :] for g in grads] + [pad], axis=0))
            mine = jnp.where(c == 0, both[0], both[1])
            theirs = jnp.where(c == 0, both[1], both[0])
            for x in range(4):
                mine_ref[x, y, half] = mine[16 * x : 16 * x + 16, :]
                theirs_ref[x, y, half] = theirs[16 * x : 16 * x + 16, :]
    for one in leave:
        one.wait()


def split_kernel(place, parts, keep_ref, give_ref):
    h = place[1]
    total = parts[0].astype(F32)
    for i in range(1, 16):
        total = total + parts[i].astype(F32)
    keep_ref[...] = jnp.where(h == 0, total[0], total[1])
    give_ref[...] = jnp.where(h == 0, total[1], total[0])


def backward_kernel(
    place, w_h, slope_h, cot_h, prev_h, next_h, far_h, grad_ref,
    w_ref, slope, cot, cot_prev, cot_next, far, windows, sems,
):
    arrive = copies(
        sems, (w_h.at[SPACE:TAPS], w_ref.at[SPACE:TAPS]), (cot_h, cot), (prev_h, cot_prev), (next_h, cot_next),
        (far_h, far), (slope_h, slope), (w_h.at[0:SPACE], w_ref.at[0:SPACE]),
    )
    for one in arrive[:5]:
        one.wait()
    before, after = sides(place, cot_prev[...], cot_next[...], far[...])
    gh = dot_nt(after, tap(w_ref, 9))
    gh = gh + dot_nt(cot[...].astype(BF), tap(w_ref, 10))
    gh = gh + dot_nt(before, tap(w_ref, 11))
    arrive[5].wait()
    gs = (gh * slope[...]).astype(BF).astype(F32)
    fill_windows(windows, gs)
    arrive[6].wait()
    acc = cot[...]
    for a in range(3):
        for b in range(3):
            acc = acc + dot_nt(windows[2 - b, (2 - a) * W : (2 - a) * W + ROWS, :], tap(w_ref, 3 * a + b))
    grad_ref[...] = acc


def output_kernel(
    place, w_h, video_h, hidden_h, prev_h, after_h, far_h, out_ref,
    w_ref, video, hidden, prev, after, far, sems,
):
    for one in copies(
        sems, (w_h.at[SPACE:TAPS], w_ref), (video_h, video), (hidden_h, hidden), (prev_h, prev), (after_h, after), (far_h, far),
    ):
        one.wait()
    before, behind = sides(place, prev[...], after[...], far[...])
    acc = video[...] + dot(hidden[...], tap(w_ref, 1))
    acc = acc + dot(before, tap(w_ref, 0))
    out_ref[...] = acc + dot(behind, tap(w_ref, 2))


FRAME_B = (ROWS, C), BF
FRAME_F = (ROWS, C), F32
WINDOWS = (3, ROWS + 2 * W, C), BF
WEIGHTS = (TAPS, 2, HALF, C), BF
SUMS = (4, 4, 2, 16, C), F32
SHARE = (16, C), F32


def kernel_call(body, ins, outs, scratch, copied, micros, name, limit=60):
    spaces = {"s": pltpu.SMEM, "v": pltpu.VMEM, "h": pltpu.HBM}
    specs = [[pl.BlockSpec(memory_space=spaces[o[-1]]) for o in group] for group in (ins, outs)]
    return pl.pallas_call(
        body,
        out_shape=tuple(jax.ShapeDtypeStruct(*o[0]) for o in outs),
        in_specs=specs[0],
        out_specs=tuple(specs[1]),
        scratch_shapes=[pltpu.VMEM(*o) for o in scratch] + [pltpu.SemaphoreType.DMA((copied,))] * (copied > 0),
        compiler_params=pltpu.CompilerParams(vmem_limit_bytes=limit * 1024 * 1024),
        cost_estimate=pl.CostEstimate(flops=int(micros * 1.0e9), bytes_accessed=1_000_000, transcendentals=0),
        name=name,
    )(*(a for a, _ in ins))


def on_device(video, spatial_w, spatial_b, temporal_w, cotangent):
    tie = lax.optimization_barrier
    c, h, x, z = (lax.axis_index(a) for a in ("c", "h", "x", Z_LO))
    wrapped = ((z == 0) & (x > 0)) | ((z == 7) & (x < 3))
    place = jnp.stack([c, h, z, wrapped.astype(jnp.int32)]).astype(jnp.int32)
    shape = video.shape
    video_f = video.reshape(ROWS, C)
    cot_f = cotangent.reshape(ROWS, C)
    bias = spatial_b.reshape(1, C)

    cot_b = cot_f.astype(BF)
    w = jnp.concatenate([spatial_w, temporal_w.astype(BF)], axis=0)
    quarter = lax.dynamic_slice_in_dim(w, 3 * x, 3, 0).reshape(3 * OWN, C)
    other = across(jnp.pad(quarter, ((0, SLOT - 3 * OWN), (0, WIDE - C))))
    w = jnp.pad(w.reshape(TAPS * OWN, C), ((0, 0), (0, WIDE - C)))
    other, cot_b, w = tie((other, cot_b, w))
    cot_next = lax.ppermute(cot_b, TM, FRAMES_DOWN)
    cot_prev = lax.ppermute(cot_b, TM, FRAMES_UP)
    far = lax.ppermute(cot_b, TM, FRAMES_FAR)
    own_m = to_all(jnp.concatenate([w, other], axis=0), "y")
    (oth_m,) = kernel_call(
        apart_kernel, [(own_m, "v")], [(((4 * SLOT, WIDE), BF), "v")], [], 0, 1000, "apart", 8,
    )
    oth_m = lax.all_gather(oth_m, "x")
    oth_m, own_m, video_w = tie((oth_m, own_m, video_f))
    oth_m, cot_next, cot_prev, far = tie((oth_m, cot_next, cot_prev, far))
    (windows,) = kernel_call(prepare_kernel, [(video_w, "v")], [(WINDOWS, "v")], [], 0, 0.01, "prepare", 16)
    own_t, oth_t = core_swap(own_m), core_swap(oth_m)

    w_all, hidden, slope, mine, theirs = kernel_call(
        forward_kernel,
        [
            (place, "s"), (own_m, "v"), (own_t, "v"), (oth_m, "v"), (oth_t, "v"), (windows, "v"), (bias, "v"),
            (cot_f, "v"), (cot_prev, "v"), (cot_next, "v"), (far, "v"),
        ],
        [(WEIGHTS, "h"), (FRAME_B, "v"), (FRAME_F, "v"), (SUMS, "v"), (SUMS, "v")],
        [WEIGHTS], 1, 0.01, "forward", LIMIT,
    )
    part = (mine + core_swap(theirs)).astype(BF)
    part = lax.all_to_all(part.reshape(16, 2, 16, C), PLANE, 0, 0, tiled=True)
    prev = lax.ppermute(hidden, TM, FRAMES_UP)
    after = lax.ppermute(hidden, TM, FRAMES_DOWN)
    hidden_far = lax.ppermute(hidden, TM, FRAMES_FAR)
    keep, give = kernel_call(
        split_kernel, [(place, "s"), (part, "v")], [(SHARE, "v"), (SHARE, "v")], [], 0, 1000, "split", 8,
    )
    give, slope = tie((give, slope))
    other = across(give)
    (grad_video,) = kernel_call(
        backward_kernel,
        [(place, "s"), (w_all, "h"), (slope, "h"), (cot_f, "h"), (cot_prev, "h"), (cot_next, "h"), (far, "h")],
        [(FRAME_F, "v")],
        [WEIGHTS, FRAME_F, FRAME_F, FRAME_B, FRAME_B, FRAME_B, WINDOWS], 7, 5, "backward",
    )
    other, grad_video = tie((other, grad_video))
    part = keep + other
    part, video_f, prev, after, hidden_far = tie((part, video_f, prev, after, hidden_far))
    part = to_all(part, Z_LO)
    (output,) = kernel_call(
        output_kernel,
        [(place, "s"), (w_all, "h"), (video_f, "h"), (hidden, "h"), (prev, "h"), (after, "h"), (hidden_far, "h")],
        [(FRAME_F, "v")],
        [((3, 2, HALF, C), BF), FRAME_F, FRAME_B, FRAME_B, FRAME_B, FRAME_B], 6, 3, "output",
    )
    part, output = tie((part, output))
    part = jnp.sum(part, axis=0)
    part = to_all(part, "x").reshape(4 * 16, C)
    total_rows = ROWS * lax.axis_size(TM) * lax.axis_size(CLIP)
    grad_temporal = part[: 3 * OWN].reshape(3, OWN, C) * (1.0 / math.sqrt(total_rows))
    return output.reshape(shape), grad_video.reshape(shape), grad_temporal


def solution(mesh):
    finer = Mesh(mesh.devices.reshape(SIZES), AXES)
    placed = (
        P(CLIP, TM, None, None, None),
        P(None, CLIP, None),
        P(),
        P(None, CLIP, None),
        P(CLIP, TM, None, None, None),
    )
    return jax.shard_map(
        on_device,
        mesh=finer,
        in_specs=placed,
        out_specs=(
            P(CLIP, TM, None, None, None),
            P(CLIP, TM, None, None, None),
            P(None, CLIP, None),
        ),
        check_vma=False,
    )
```

```python
import math

import jax
import jax.numpy as jnp
from jax import lax
from jax.experimental import pallas as pl
from jax.experimental.pallas import tpu as pltpu
from jax.sharding import Mesh
from jax.sharding import PartitionSpec as P

AXES = ("x", "m", "k", "h", "y", "c")
SIZES = (4, 2, 4, 2, 4, 2)
TM = ("x", "m", "k")
Z_LO = ("m", "k")
CLIP = ("h", "y", "c")
PLANE = ("x", "y")
H, W, C = 16, 32, 320
ROWS = H * W
HALF, PART, OWN = 160, 40, 20
TAPS = 12
SPACE = 9
WIDE = 384
LIMIT = 48
SLOT = 64
BF = jnp.bfloat16
F32 = jnp.float32


def pairs_across():
    def place(z):
        return (z % 8) * 2 + z // 8

    there = [(z - 4) % 16 if z % 8 < 4 else (z + 4) % 16 for z in range(16)]
    return [(place(z), place(there[z])) for z in range(16)]


ACROSS = pairs_across()
FRAMES_UP = [(t, t + 1) for t in range(31) if t % 8 != 7]
FRAMES_DOWN = [(u, t) for t, u in FRAMES_UP]
FRAMES_FAR = [p for t in (7, 15, 23) for p in ((t, t + 1), (t + 1, t))]


def across(a):
    return lax.ppermute(a, ("m", "k", "h"), ACROSS)


def core_swap(a):
    return lax.ppermute(a, "c", [(0, 1), (1, 0)])


def to_all(a, axes):
    n = lax.axis_size(axes)
    return lax.all_to_all(jnp.broadcast_to(a[None], (n, *a.shape)), axes, 0, 0, tiled=True)


def dot(a, b):
    return lax.dot_general(a, b, (((1,), (0,)), ((), ())), preferred_element_type=F32)


def dot_nt(a, b):
    return lax.dot_general(a, b, (((1,), (1,)), ((), ())), preferred_element_type=F32)


def fill_windows(windows, value):
    col = lax.broadcasted_iota(jnp.int32, (ROWS, 1), 0) % W
    edge = jnp.zeros((W, 3 * C), BF)
    windows[0:W, :] = edge
    windows[W + ROWS : 2 * W + ROWS, :] = edge
    left = jnp.where(col == 0, 0.0, pltpu.roll(value, 1, 0))
    right = jnp.where(col == W - 1, 0.0, pltpu.roll(value, ROWS - 1, 0))
    windows[W : W + ROWS, :] = jnp.concatenate([a.astype(BF) for a in (left, value, right)], axis=1)


def fill_shifts(windows, value):
    col = lax.broadcasted_iota(jnp.int32, (ROWS, 1), 0) % W
    edge = jnp.zeros((W, C), BF)
    for d in range(3):
        windows[d, 0:W, :] = edge
        windows[d, W + ROWS : 2 * W + ROWS, :] = edge
    windows[1, W : W + ROWS, :] = value.astype(BF)
    left = jnp.where(col == 0, 0.0, pltpu.roll(value, 1, 0))
    windows[0, W : W + ROWS, :] = left.astype(BF)
    right = jnp.where(col == W - 1, 0.0, pltpu.roll(value, ROWS - 1, 0))
    windows[2, W : W + ROWS, :] = right.astype(BF)


def tap(w_ref, t):
    return w_ref[t].reshape(C, C)


def join(w_ref, t, half, y, mine, theirs, c):
    low = jnp.where(c == 0, mine, theirs)
    high = jnp.where(c == 0, theirs, mine)
    w_ref[t, half, y * PART : (y + 1) * PART, :] = jnp.concatenate([low, high], axis=0)


def sides(place, before, after, far):
    first, last = place[2] == 0, place[2] == 7
    return jnp.where(first, far, before), jnp.where(last, far, after)


def conv(windows, w_ref, bias):
    acc = jnp.zeros((ROWS, C), F32) + bias
    for a in range(3):
        acc = acc + dot(windows[a * W : a * W + ROWS, :], w_ref[3 * a : 3 * a + 3].reshape(3 * C, C))
    return acc


def copies(sems, *pairs):
    started = [pltpu.make_async_copy(src, dst, sems.at[i]) for i, (src, dst) in enumerate(pairs)]
    for one in started:
        one.start()
    return started


def prepare_kernel(video, windows):
    fill_windows(windows, video[...])


def cast_kernel(cot, video, cot_out, both):
    cot_b = cot[...].astype(BF)
    cot_out[...] = cot_b
    both[0:ROWS, 0:C] = cot_b
    both[ROWS:, 0:C] = video[...].astype(BF)
    both[:, C:WIDE] = jnp.zeros((2 * ROWS, WIDE - C), BF)


def pack_kernel(spatial, temporal, other, out):
    for t in range(TAPS):
        rows = spatial[t] if t < SPACE else temporal[t - SPACE].astype(BF)
        for y in range(4):
            out[y, t * OWN : (t + 1) * OWN, 0:C] = rows
    side = jnp.zeros((TAPS * OWN, WIDE - C), BF)
    for y in range(4):
        out[y, 0 : TAPS * OWN, C:WIDE] = side
        out[y, TAPS * OWN :, :] = other[...]


def apart_kernel(gathered, out):
    for y in range(4):
        out[y * SLOT : (y + 1) * SLOT, :] = gathered[y, TAPS * OWN : TAPS * OWN + SLOT, :]


def forward_kernel(
    place, own_m, own_t, oth_m, oth_t, windows, bias, cot, cot_prev, cot_next, far,
    w_h, hidden_ref, slope_ref, mine_ref, theirs_ref, w_ref, sems,
):
    c, h = place[0], place[1]
    for t in range(TAPS):
        for y in range(4):
            at = t * OWN
            join(w_ref, t, h, y, own_m[y, at : at + OWN, 0:C], own_t[y, at : at + OWN, 0:C], c)
            x, at = t // 3, y * SLOT + (t % 3) * OWN
            join(w_ref, t, 1 - h, y, oth_m[x, at : at + OWN, 0:C], oth_t[x, at : at + OWN, 0:C], c)
    leave = copies(sems, (w_ref, w_h))
    spatial = conv(windows, w_ref, bias[...])
    sig = jax.nn.sigmoid(spatial)
    hidden = (spatial * sig).astype(BF)
    hidden_ref[...] = hidden
    slope_ref[...] = sig * (1.0 + spatial * (1.0 - sig))
    before, after = sides(place, cot_prev[...], cot_next[...], far[0:ROWS, 0:C])
    turned = hidden.T
    grads = [dot(turned, other) for other in (after, cot[...].astype(BF), before)]
    pad = jnp.zeros((4, C), F32)
    for half in range(2):
        for y in range(4):
            both = []
            for core in range(2):
                r = half * HALF + y * PART + core * OWN
                both.append(jnp.concatenate([g[r : r + OWN, :] for g in grads] + [pad], axis=0))
            mine = jnp.where(c == 0, both[0], both[1])
            theirs = jnp.where(c == 0, both[1], both[0])
            for x in range(4):
                mine_ref[x, y, half] = mine[16 * x : 16 * x + 16, :]
                theirs_ref[x, y, half] = theirs[16 * x : 16 * x + 16, :]
    for one in leave:
        one.wait()


def split_kernel(place, parts, keep_ref, give_ref):
    h = place[1]
    total = parts[0].astype(F32)
    for i in range(1, 16):
        total = total + parts[i].astype(F32)
    keep_ref[...] = jnp.where(h == 0, total[0], total[1])
    give_ref[...] = jnp.where(h == 0, total[1], total[0])


def backward_kernel(
    place, w_h, slope_h, cot_h, prev_h, next_h, far_h, grad_ref,
    w_ref, slope, cot, cot_prev, cot_next, far, windows, sems,
):
    arrive = copies(
        sems, (w_h.at[SPACE:TAPS], w_ref.at[SPACE:TAPS]), (cot_h, cot), (prev_h, cot_prev), (next_h, cot_next),
        (far_h.at[0:ROWS, :], far), (slope_h, slope), (w_h.at[0:SPACE], w_ref.at[0:SPACE]),
    )
    for one in arrive[:5]:
        one.wait()
    before, after = sides(place, cot_prev[...], cot_next[...], far[0:ROWS, 0:C])
    gh = dot_nt(after, tap(w_ref, 9))
    gh = gh + dot_nt(cot[...].astype(BF), tap(w_ref, 10))
    gh = gh + dot_nt(before, tap(w_ref, 11))
    arrive[5].wait()
    gs = (gh * slope[...]).astype(BF).astype(F32)
    fill_shifts(windows, gs)
    arrive[6].wait()
    acc = cot[...]
    for a in range(3):
        for b in range(3):
            acc = acc + dot_nt(windows[2 - b, (2 - a) * W : (2 - a) * W + ROWS, :], tap(w_ref, 3 * a + b))
    grad_ref[...] = acc


def far_kernel(place, w_h, far_h, bias, hidden_h, w_ref, far, hidden_ref, windows, sems):
    arrive = copies(sems, (far_h.at[ROWS : 2 * ROWS, :], far), (w_h.at[0:SPACE], w_ref))
    arrive[0].wait()
    fill_windows(windows, far[:, 0:C].astype(F32))
    arrive[1].wait()
    spatial = conv(windows, w_ref, bias[...])
    hidden = (spatial * jax.nn.sigmoid(spatial)).astype(BF)
    hidden_ref[...] = jnp.where(place[3] == 1, hidden, jnp.zeros_like(hidden))
    for one in copies(sems, (hidden_ref, hidden_h)):
        one.wait()


def output_kernel(
    place, w_h, video_h, hidden_h, prev_h, after_h, far_h, out_ref,
    w_ref, video, hidden, prev, after, far, sems,
):
    for one in copies(
        sems, (w_h.at[SPACE:TAPS], w_ref), (video_h, video), (hidden_h, hidden), (prev_h, prev), (after_h, after), (far_h, far),
    ):
        one.wait()
    before, behind = sides(place, prev[...], after[...], far[...])
    acc = video[...] + dot(hidden[...], tap(w_ref, 1))
    acc = acc + dot(before, tap(w_ref, 0))
    out_ref[...] = acc + dot(behind, tap(w_ref, 2))


FRAME_B = (ROWS, C), BF
FRAME_F = (ROWS, C), F32
WINDOWS = (ROWS + 2 * W, 3 * C), BF
SHIFTS = (3, ROWS + 2 * W, C), BF
WEIGHTS = (TAPS, 2, HALF, C), BF
SUMS = (4, 4, 2, 16, C), F32
SHARE = (16, C), F32


def kernel_call(body, ins, outs, scratch, copied, micros, name, limit=60):
    spaces = {"s": pltpu.SMEM, "v": pltpu.VMEM, "h": pltpu.HBM}
    specs = [[pl.BlockSpec(memory_space=spaces[o[-1]]) for o in group] for group in (ins, outs)]
    return pl.pallas_call(
        body,
        out_shape=tuple(jax.ShapeDtypeStruct(*o[0]) for o in outs),
        in_specs=specs[0],
        out_specs=tuple(specs[1]),
        scratch_shapes=[pltpu.VMEM(*o) for o in scratch] + [pltpu.SemaphoreType.DMA((copied,))] * (copied > 0),
        compiler_params=pltpu.CompilerParams(vmem_limit_bytes=limit * 1024 * 1024),
        cost_estimate=pl.CostEstimate(flops=int(micros * 1.0e9), bytes_accessed=1_000_000, transcendentals=0),
        name=name,
    )(*(a for a, _ in ins))


def on_device(video, spatial_w, spatial_b, temporal_w, cotangent):
    tie = lax.optimization_barrier
    c, h, x, z = (lax.axis_index(a) for a in ("c", "h", "x", Z_LO))
    wrapped = ((z == 0) & (x > 0)) | ((z == 7) & (x < 3))
    place = jnp.stack([c, h, z, wrapped.astype(jnp.int32)]).astype(jnp.int32)
    shape = video.shape
    video_f = video.reshape(ROWS, C)
    cot_f = cotangent.reshape(ROWS, C)
    bias = spatial_b.reshape(1, C)

    w = jnp.concatenate([spatial_w, temporal_w.astype(BF)], axis=0)
    quarter = lax.dynamic_slice_in_dim(w, 3 * x, 3, 0).reshape(3 * OWN, C)
    other = across(jnp.pad(quarter, ((0, SLOT - 3 * OWN), (0, WIDE - C))))
    other, cot_w, video_w = tie((other, cot_f, video_f))
    cot_b, both = kernel_call(
        cast_kernel, [(cot_w, "v"), (video_w, "v")], [(FRAME_B, "v"), (((2 * ROWS, WIDE), BF), "v")], [], 0, 0.01, "cast", 8,
    )
    cot_next = lax.ppermute(cot_b, TM, FRAMES_DOWN)
    cot_prev = lax.ppermute(cot_b, TM, FRAMES_UP)
    far = lax.ppermute(both, TM, FRAMES_FAR)
    (packed,) = kernel_call(
        pack_kernel, [(spatial_w, "v"), (temporal_w, "v"), (other, "v")], [(((4, TAPS * OWN + SLOT, WIDE), BF), "v")],
        [], 0, 0.01, "pack", 8,
    )
    own_m = lax.all_to_all(packed, "y", 0, 0, tiled=True)
    (oth_m,) = kernel_call(
        apart_kernel, [(own_m, "v")], [(((4 * SLOT, WIDE), BF), "v")], [], 0, 1000, "apart", 8,
    )
    oth_m = lax.all_gather(oth_m, "x")
    oth_m, own_m, video_w = tie((oth_m, own_m, video_f))
    oth_m, cot_next, cot_prev, far = tie((oth_m, cot_next, cot_prev, far))
    (windows,) = kernel_call(prepare_kernel, [(video_w, "v")], [(WINDOWS, "v")], [], 0, 0.01, "prepare", 16)
    own_t, oth_t = core_swap(own_m), core_swap(oth_m)

    w_all, hidden, slope, mine, theirs = kernel_call(
        forward_kernel,
        [
            (place, "s"), (own_m, "v"), (own_t, "v"), (oth_m, "v"), (oth_t, "v"), (windows, "v"), (bias, "v"),
            (cot_f, "v"), (cot_prev, "v"), (cot_next, "v"), (far, "v"),
        ],
        [(WEIGHTS, "h"), (FRAME_B, "v"), (FRAME_F, "v"), (SUMS, "v"), (SUMS, "v")],
        [WEIGHTS], 1, 0.01, "forward", LIMIT,
    )
    part = (mine + core_swap(theirs)).astype(BF)
    part = lax.all_to_all(part.reshape(16, 2, 16, C), PLANE, 0, 0, tiled=True)
    prev = lax.ppermute(hidden, TM, FRAMES_UP)
    after = lax.ppermute(hidden, TM, FRAMES_DOWN)
    (hidden_far,) = kernel_call(
        far_kernel, [(place, "s"), (w_all, "h"), (far, "h"), (bias, "v")], [(FRAME_B, "h")],
        [((SPACE, 2, HALF, C), BF), ((ROWS, WIDE), BF), FRAME_B, WINDOWS], 2, 0.01, "far",
    )
    part, hidden_far = tie((part, hidden_far))
    keep, give = kernel_call(
        split_kernel, [(place, "s"), (part, "v")], [(SHARE, "v"), (SHARE, "v")], [], 0, 1000, "split", 8,
    )
    give, slope = tie((give, slope))
    other = across(give)
    (grad_video,) = kernel_call(
        backward_kernel,
        [(place, "s"), (w_all, "h"), (slope, "h"), (cot_f, "h"), (cot_prev, "h"), (cot_next, "h"), (far, "h")],
        [(FRAME_F, "v")],
        [WEIGHTS, FRAME_F, FRAME_F, FRAME_B, FRAME_B, ((ROWS, WIDE), BF), SHIFTS], 7, 5, "backward",
    )
    other, grad_video = tie((other, grad_video))
    part = keep + other
    part, video_f, prev, after, hidden_far = tie((part, video_f, prev, after, hidden_far))
    part = to_all(part, Z_LO)
    (output,) = kernel_call(
        output_kernel,
        [(place, "s"), (w_all, "h"), (video_f, "h"), (hidden, "h"), (prev, "h"), (after, "h"), (hidden_far, "h")],
        [(FRAME_F, "v")],
        [((3, 2, HALF, C), BF), FRAME_F, FRAME_B, FRAME_B, FRAME_B, FRAME_B], 6, 3, "output",
    )
    part, output = tie((part, output))
    part = jnp.sum(part, axis=0)
    part = to_all(part, "x").reshape(4 * 16, C)
    total_rows = ROWS * lax.axis_size(TM) * lax.axis_size(CLIP)
    grad_temporal = part[: 3 * OWN].reshape(3, OWN, C) * (1.0 / math.sqrt(total_rows))
    return output.reshape(shape), grad_video.reshape(shape), grad_temporal


def solution(mesh):
    finer = Mesh(mesh.devices.reshape(SIZES), AXES)
    placed = (
        P(CLIP, TM, None, None, None),
        P(None, CLIP, None),
        P(),
        P(None, CLIP, None),
        P(CLIP, TM, None, None, None),
    )
    return jax.shard_map(
        on_device,
        mesh=finer,
        in_specs=placed,
        out_specs=(
            P(CLIP, TM, None, None, None),
            P(CLIP, TM, None, None, None),
            P(None, CLIP, None),
        ),
        check_vma=False,
    )
```

```python
import math

import jax
import jax.numpy as jnp
from jax import lax
from jax.experimental import pallas as pl
from jax.experimental.pallas import tpu as pltpu
from jax.sharding import Mesh
from jax.sharding import PartitionSpec as P

AXES = ("x", "m", "k", "h", "y", "c")
SIZES = (4, 2, 4, 2, 4, 2)
TM = ("x", "m", "k")
Z_LO = ("m", "k")
CLIP = ("h", "y", "c")
PLANE = ("x", "y")
H, W, C = 16, 32, 320
ROWS = H * W
HALF, PART, OWN = 160, 40, 20
TAPS = 12
SPACE = 9
WIDE = 384
LIMIT = 48
SLOT = 64
BF = jnp.bfloat16
F32 = jnp.float32


def pairs_across():
    def place(z):
        return (z % 8) * 2 + z // 8

    there = [(z - 4) % 16 if z % 8 < 4 else (z + 4) % 16 for z in range(16)]
    return [(place(z), place(there[z])) for z in range(16)]


ACROSS = pairs_across()
FRAMES_UP = [(t, t + 1) for t in range(31) if t % 8 != 7]
FRAMES_DOWN = [(u, t) for t, u in FRAMES_UP]
FRAMES_FAR = [p for t in (7, 15, 23) for p in ((t, t + 1), (t + 1, t))]


def across(a):
    return lax.ppermute(a, ("m", "k", "h"), ACROSS)


def core_swap(a):
    return lax.ppermute(a, "c", [(0, 1), (1, 0)])


def to_all(a, axes):
    n = lax.axis_size(axes)
    return lax.all_to_all(jnp.broadcast_to(a[None], (n, *a.shape)), axes, 0, 0, tiled=True)


def dot(a, b):
    return lax.dot_general(a, b, (((1,), (0,)), ((), ())), preferred_element_type=F32)


def dot_nt(a, b):
    return lax.dot_general(a, b, (((1,), (1,)), ((), ())), preferred_element_type=F32)


def fill_windows(windows, value):
    col = lax.broadcasted_iota(jnp.int32, (ROWS, 1), 0) % W
    edge = jnp.zeros((W, 3 * C), BF)
    windows[0:W, :] = edge
    windows[W + ROWS : 2 * W + ROWS, :] = edge
    left = jnp.where(col == 0, 0.0, pltpu.roll(value, 1, 0))
    right = jnp.where(col == W - 1, 0.0, pltpu.roll(value, ROWS - 1, 0))
    windows[W : W + ROWS, :] = jnp.concatenate([a.astype(BF) for a in (left, value, right)], axis=1)


def fill_shifts(windows, value):
    col = lax.broadcasted_iota(jnp.int32, (ROWS, 1), 0) % W
    edge = jnp.zeros((W, C), BF)
    for d in range(3):
        windows[d, 0:W, :] = edge
        windows[d, W + ROWS : 2 * W + ROWS, :] = edge
    windows[1, W : W + ROWS, :] = value.astype(BF)
    left = jnp.where(col == 0, 0.0, pltpu.roll(value, 1, 0))
    windows[0, W : W + ROWS, :] = left.astype(BF)
    right = jnp.where(col == W - 1, 0.0, pltpu.roll(value, ROWS - 1, 0))
    windows[2, W : W + ROWS, :] = right.astype(BF)


def tap(w_ref, t):
    return w_ref[t].reshape(C, C)


def join(w_ref, t, half, y, mine, theirs, c):
    low = jnp.where(c == 0, mine, theirs)
    high = jnp.where(c == 0, theirs, mine)
    w_ref[t, half, y * PART : (y + 1) * PART, :] = jnp.concatenate([low, high], axis=0)


def sides(place, before, after, far):
    first, last = place[2] == 0, place[2] == 7
    return jnp.where(first, far, before), jnp.where(last, far, after)


def conv(windows, w_ref, bias):
    acc = jnp.zeros((ROWS, C), F32) + bias
    for a in range(3):
        acc = acc + dot(windows[a * W : a * W + ROWS, :], w_ref[3 * a : 3 * a + 3].reshape(3 * C, C))
    return acc


def copies(sems, *pairs):
    started = [pltpu.make_async_copy(src, dst, sems.at[i]) for i, (src, dst) in enumerate(pairs)]
    for one in started:
        one.start()
    return started


def prepare_kernel(video, windows):
    fill_windows(windows, video[...])


def apart_kernel(gathered, out):
    for y in range(4):
        out[y * SLOT : (y + 1) * SLOT, :] = gathered[y, TAPS * OWN : TAPS * OWN + SLOT, :]


def forward_kernel(
    place, own_m, own_t, oth_m, oth_t, windows, bias, cot, cot_prev, cot_next, far,
    w_h, hidden_ref, slope_ref, mine_ref, theirs_ref, w_ref, sems,
):
    c, h = place[0], place[1]
    for t in range(TAPS):
        for y in range(4):
            at = t * OWN
            join(w_ref, t, h, y, own_m[y, at : at + OWN, 0:C], own_t[y, at : at + OWN, 0:C], c)
            x, at = t // 3, y * SLOT + (t % 3) * OWN
            join(w_ref, t, 1 - h, y, oth_m[x, at : at + OWN, 0:C], oth_t[x, at : at + OWN, 0:C], c)
    leave = copies(sems, (w_ref, w_h))
    spatial = conv(windows, w_ref, bias[...])
    sig = jax.nn.sigmoid(spatial)
    hidden = (spatial * sig).astype(BF)
    hidden_ref[...] = hidden
    slope_ref[...] = sig * (1.0 + spatial * (1.0 - sig))
    before, after = sides(place, cot_prev[...], cot_next[...], far[...])
    turned = hidden.T
    grads = [dot(turned, other) for other in (after, cot[...].astype(BF), before)]
    pad = jnp.zeros((4, C), F32)
    for half in range(2):
        for y in range(4):
            both = []
            for core in range(2):
                r = half * HALF + y * PART + core * OWN
                both.append(jnp.concatenate([g[r : r + OWN, :] for g in grads] + [pad], axis=0))
            mine = jnp.where(c == 0, both[0], both[1])
            theirs = jnp.where(c == 0, both[1], both[0])
            for x in range(4):
                mine_ref[x, y, half] = mine[16 * x : 16 * x + 16, :]
                theirs_ref[x, y, half] = theirs[16 * x : 16 * x + 16, :]
    for one in leave:
        one.wait()


def split_kernel(place, parts, keep_ref, give_ref):
    h = place[1]
    total = parts[0].astype(F32)
    for i in range(1, 16):
        total = total + parts[i].astype(F32)
    keep_ref[...] = jnp.where(h == 0, total[0], total[1])
    give_ref[...] = jnp.where(h == 0, total[1], total[0])


def backward_kernel(
    place, w_h, slope_h, cot_h, prev_h, next_h, far_h, grad_ref,
    w_ref, slope, cot, cot_prev, cot_next, far, windows, sems,
):
    arrive = copies(
        sems, (w_h.at[SPACE:TAPS], w_ref.at[SPACE:TAPS]), (cot_h, cot), (prev_h, cot_prev), (next_h, cot_next),
        (far_h, far), (slope_h, slope), (w_h.at[0:SPACE], w_ref.at[0:SPACE]),
    )
    for one in arrive[:5]:
        one.wait()
    before, after = sides(place, cot_prev[...], cot_next[...], far[...])
    gh = dot_nt(after, tap(w_ref, 9))
    gh = gh + dot_nt(cot[...].astype(BF), tap(w_ref, 10))
    gh = gh + dot_nt(before, tap(w_ref, 11))
    arrive[5].wait()
    gs = (gh * slope[...]).astype(BF).astype(F32)
    fill_shifts(windows, gs)
    arrive[6].wait()
    acc = cot[...]
    for a in range(3):
        for b in range(3):
            acc = acc + dot_nt(windows[2 - b, (2 - a) * W : (2 - a) * W + ROWS, :], tap(w_ref, 3 * a + b))
    grad_ref[...] = acc


def output_kernel(
    place, w_h, video_h, hidden_h, prev_h, after_h, far_h, out_ref,
    w_ref, video, hidden, prev, after, far, sems,
):
    for one in copies(
        sems, (w_h.at[SPACE:TAPS], w_ref), (video_h, video), (hidden_h, hidden), (prev_h, prev), (after_h, after), (far_h, far),
    ):
        one.wait()
    before, behind = sides(place, prev[...], after[...], far[...])
    acc = video[...] + dot(hidden[...], tap(w_ref, 1))
    acc = acc + dot(before, tap(w_ref, 0))
    out_ref[...] = acc + dot(behind, tap(w_ref, 2))


FRAME_B = (ROWS, C), BF
FRAME_F = (ROWS, C), F32
WINDOWS = (ROWS + 2 * W, 3 * C), BF
SHIFTS = (3, ROWS + 2 * W, C), BF
WEIGHTS = (TAPS, 2, HALF, C), BF
SUMS = (4, 4, 2, 16, C), F32
SHARE = (16, C), F32


def kernel_call(body, ins, outs, scratch, copied, micros, name, limit=60):
    spaces = {"s": pltpu.SMEM, "v": pltpu.VMEM, "h": pltpu.HBM}
    specs = [[pl.BlockSpec(memory_space=spaces[o[-1]]) for o in group] for group in (ins, outs)]
    return pl.pallas_call(
        body,
        out_shape=tuple(jax.ShapeDtypeStruct(*o[0]) for o in outs),
        in_specs=specs[0],
        out_specs=tuple(specs[1]),
        scratch_shapes=[pltpu.VMEM(*o) for o in scratch] + [pltpu.SemaphoreType.DMA((copied,))] * (copied > 0),
        compiler_params=pltpu.CompilerParams(vmem_limit_bytes=limit * 1024 * 1024),
        cost_estimate=pl.CostEstimate(flops=int(micros * 1.0e9), bytes_accessed=1_000_000, transcendentals=0),
        name=name,
    )(*(a for a, _ in ins))


def on_device(video, spatial_w, spatial_b, temporal_w, cotangent):
    tie = lax.optimization_barrier
    c, h, x, z = (lax.axis_index(a) for a in ("c", "h", "x", Z_LO))
    wrapped = ((z == 0) & (x > 0)) | ((z == 7) & (x < 3))
    place = jnp.stack([c, h, z, wrapped.astype(jnp.int32)]).astype(jnp.int32)
    shape = video.shape
    video_f = video.reshape(ROWS, C)
    cot_f = cotangent.reshape(ROWS, C)
    bias = spatial_b.reshape(1, C)

    cot_b = cot_f.astype(BF)
    w = jnp.concatenate([spatial_w, temporal_w.astype(BF)], axis=0)
    quarter = lax.dynamic_slice_in_dim(w, 3 * x, 3, 0).reshape(3 * OWN, C)
    other = across(jnp.pad(quarter, ((0, SLOT - 3 * OWN), (0, WIDE - C))))
    w = jnp.pad(w.reshape(TAPS * OWN, C), ((0, 0), (0, WIDE - C)))
    other, cot_b, w = tie((other, cot_b, w))
    far = lax.ppermute(cot_b, TM, FRAMES_FAR)
    cot_next = lax.ppermute(cot_b, TM, FRAMES_DOWN)
    cot_prev = lax.ppermute(cot_b, TM, FRAMES_UP)
    own_m = to_all(jnp.concatenate([w, other], axis=0), "y")
    (oth_m,) = kernel_call(
        apart_kernel, [(own_m, "v")], [(((4 * SLOT, WIDE), BF), "v")], [], 0, 1000, "apart", 8,
    )
    oth_m = lax.all_gather(oth_m, "x")
    oth_m, own_m, video_w = tie((oth_m, own_m, video_f))
    far, oth_m, cot_next, cot_prev = tie((far, oth_m, cot_next, cot_prev))
    (windows,) = kernel_call(prepare_kernel, [(video_w, "v")], [(WINDOWS, "v")], [], 0, 0.01, "prepare", 16)
    own_t, oth_t = core_swap(own_m), core_swap(oth_m)

    w_all, hidden, slope, mine, theirs = kernel_call(
        forward_kernel,
        [
            (place, "s"), (own_m, "v"), (own_t, "v"), (oth_m, "v"), (oth_t, "v"), (windows, "v"), (bias, "v"),
            (cot_f, "v"), (cot_prev, "v"), (cot_next, "v"), (far, "v"),
        ],
        [(WEIGHTS, "h"), (FRAME_B, "v"), (FRAME_F, "v"), (SUMS, "v"), (SUMS, "v")],
        [WEIGHTS], 1, 0.01, "forward", LIMIT,
    )
    part = (mine + core_swap(theirs)).astype(BF)
    part = lax.all_to_all(part.reshape(16, 2, 16, C), PLANE, 0, 0, tiled=True)
    hidden_far = lax.ppermute(hidden, TM, FRAMES_FAR)
    prev = lax.ppermute(hidden, TM, FRAMES_UP)
    after = lax.ppermute(hidden, TM, FRAMES_DOWN)
    keep, give = kernel_call(
        split_kernel, [(place, "s"), (part, "v")], [(SHARE, "v"), (SHARE, "v")], [], 0, 1000, "split", 8,
    )
    give, slope = tie((give, slope))
    other = across(give)
    (grad_video,) = kernel_call(
        backward_kernel,
        [(place, "s"), (w_all, "h"), (slope, "h"), (cot_f, "h"), (cot_prev, "h"), (cot_next, "h"), (far, "h")],
        [(FRAME_F, "v")],
        [WEIGHTS, FRAME_F, FRAME_F, FRAME_B, FRAME_B, FRAME_B, SHIFTS], 7, 5, "backward",
    )
    other, grad_video = tie((other, grad_video))
    part = keep + other
    hidden_far, part, video_f, prev, after = tie((hidden_far, part, video_f, prev, after))
    part = to_all(part, Z_LO)
    (output,) = kernel_call(
        output_kernel,
        [(place, "s"), (w_all, "h"), (video_f, "h"), (hidden, "h"), (prev, "h"), (after, "h"), (hidden_far, "h")],
        [(FRAME_F, "v")],
        [((3, 2, HALF, C), BF), FRAME_F, FRAME_B, FRAME_B, FRAME_B, FRAME_B], 6, 3, "output",
    )
    part, output = tie((part, output))
    part = jnp.sum(part, axis=0)
    part = to_all(part, "x").reshape(4 * 16, C)
    total_rows = ROWS * lax.axis_size(TM) * lax.axis_size(CLIP)
    grad_temporal = part[: 3 * OWN].reshape(3, OWN, C) * (1.0 / math.sqrt(total_rows))
    return output.reshape(shape), grad_video.reshape(shape), grad_temporal


def solution(mesh):
    finer = Mesh(mesh.devices.reshape(SIZES), AXES)
    placed = (
        P(CLIP, TM, None, None, None),
        P(None, CLIP, None),
        P(),
        P(None, CLIP, None),
        P(CLIP, TM, None, None, None),
    )
    return jax.shard_map(
        on_device,
        mesh=finer,
        in_specs=placed,
        out_specs=(
            P(CLIP, TM, None, None, None),
            P(CLIP, TM, None, None, None),
            P(None, CLIP, None),
        ),
        check_vma=False,
    )
```

```python
import math

import jax
import jax.numpy as jnp
from jax import lax
from jax.experimental import pallas as pl
from jax.experimental.pallas import tpu as pltpu
from jax.sharding import Mesh
from jax.sharding import PartitionSpec as P

AXES = ("x", "m", "k", "h", "y", "c")
SIZES = (4, 2, 4, 2, 4, 2)
TM = ("x", "m", "k")
Z_LO = ("m", "k")
CLIP = ("h", "y", "c")
PLANE = ("x", "y")
H, W, C = 16, 32, 320
ROWS = H * W
HALF, PART, OWN = 160, 40, 20
TAPS = 12
SPACE = 9
WIDE = 384
LIMIT = 48
SLOT = 64
BF = jnp.bfloat16
F32 = jnp.float32


def pairs_across():
    def place(z):
        return (z % 8) * 2 + z // 8

    there = [(z - 4) % 16 if z % 8 < 4 else (z + 4) % 16 for z in range(16)]
    return [(place(z), place(there[z])) for z in range(16)]


ACROSS = pairs_across()
FRAMES_UP = [(t, t + 1) for t in range(31) if t % 8 != 7]
FRAMES_DOWN = [(u, t) for t, u in FRAMES_UP]
FRAMES_FAR = [p for t in (7, 15, 23) for p in ((t, t + 1), (t + 1, t))]


def across(a):
    return lax.ppermute(a, ("m", "k", "h"), ACROSS)


def core_swap(a):
    return lax.ppermute(a, "c", [(0, 1), (1, 0)])


def to_all(a, axes):
    n = lax.axis_size(axes)
    return lax.all_to_all(jnp.broadcast_to(a[None], (n, *a.shape)), axes, 0, 0, tiled=True)


def dot(a, b):
    return lax.dot_general(a, b, (((1,), (0,)), ((), ())), preferred_element_type=F32)


def dot_nt(a, b):
    return lax.dot_general(a, b, (((1,), (1,)), ((), ())), preferred_element_type=F32)


def fill_windows(windows, value):
    col = lax.broadcasted_iota(jnp.int32, (ROWS, 1), 0) % W
    edge = jnp.zeros((W, 3 * C), BF)
    windows[0:W, :] = edge
    windows[W + ROWS : 2 * W + ROWS, :] = edge
    left = jnp.where(col == 0, 0.0, pltpu.roll(value, 1, 0))
    right = jnp.where(col == W - 1, 0.0, pltpu.roll(value, ROWS - 1, 0))
    windows[W : W + ROWS, :] = jnp.concatenate([a.astype(BF) for a in (left, value, right)], axis=1)


def fill_shifts(windows, value):
    col = lax.broadcasted_iota(jnp.int32, (ROWS, 1), 0) % W
    edge = jnp.zeros((W, C), BF)
    for d in range(3):
        windows[d, 0:W, :] = edge
        windows[d, W + ROWS : 2 * W + ROWS, :] = edge
    windows[1, W : W + ROWS, :] = value.astype(BF)
    left = jnp.where(col == 0, 0.0, pltpu.roll(value, 1, 0))
    windows[0, W : W + ROWS, :] = left.astype(BF)
    right = jnp.where(col == W - 1, 0.0, pltpu.roll(value, ROWS - 1, 0))
    windows[2, W : W + ROWS, :] = right.astype(BF)


def tap(w_ref, t):
    return w_ref[t].reshape(C, C)


def join(w_ref, t, half, y, mine, theirs, c):
    low = jnp.where(c == 0, mine, theirs)
    high = jnp.where(c == 0, theirs, mine)
    w_ref[t, half, y * PART : (y + 1) * PART, :] = jnp.concatenate([low, high], axis=0)


def sides(place, before, after, far):
    first, last = place[2] == 0, place[2] == 7
    return jnp.where(first, far, before), jnp.where(last, far, after)


def conv(windows, w_ref, bias):
    acc = jnp.zeros((ROWS, C), F32) + bias
    for a in range(3):
        acc = acc + dot(windows[a * W : a * W + ROWS, :], w_ref[3 * a : 3 * a + 3].reshape(3 * C, C))
    return acc


def copies(sems, *pairs):
    started = [pltpu.make_async_copy(src, dst, sems.at[i]) for i, (src, dst) in enumerate(pairs)]
    for one in started:
        one.start()
    return started


def prepare_kernel(video, windows):
    fill_windows(windows, video[...])


def apart_kernel(gathered, out):
    for y in range(4):
        out[y * SLOT : (y + 1) * SLOT, :] = gathered[y, TAPS * OWN : TAPS * OWN + SLOT, :]


def forward_kernel(
    place, own_m, own_t, oth_m, oth_t, windows, bias, cot, cot_prev, cot_next, far,
    w_h, hidden_ref, slope_ref, mine_ref, theirs_ref, w_ref, sems,
):
    c, h = place[0], place[1]
    for t in range(TAPS):
        for y in range(4):
            at = t * OWN
            join(w_ref, t, h, y, own_m[y, at : at + OWN, 0:C], own_t[y, at : at + OWN, 0:C], c)
            x, at = t // 3, y * SLOT + (t % 3) * OWN
            join(w_ref, t, 1 - h, y, oth_m[x, at : at + OWN, 0:C], oth_t[x, at : at + OWN, 0:C], c)
    leave = copies(sems, (w_ref, w_h))
    spatial = conv(windows, w_ref, bias[...])
    sig = jax.nn.sigmoid(spatial)
    hidden = (spatial * sig).astype(BF)
    hidden_ref[...] = hidden
    slope_ref[...] = sig * (1.0 + spatial * (1.0 - sig))
    before, after = sides(place, cot_prev[...], cot_next[...], far[...])
    turned = hidden.T
    grads = [dot(turned, other) for other in (after, cot[...].astype(BF), before)]
    pad = jnp.zeros((4, C), F32)
    for half in range(2):
        for y in range(4):
            both = []
            for core in range(2):
                r = half * HALF + y * PART + core * OWN
                both.append(jnp.concatenate([g[r : r + OWN, :] for g in grads] + [pad], axis=0))
            mine = jnp.where(c == 0, both[0], both[1])
            theirs = jnp.where(c == 0, both[1], both[0])
            for x in range(4):
                mine_ref[x, y, half] = mine[16 * x : 16 * x + 16, :]
                theirs_ref[x, y, half] = theirs[16 * x : 16 * x + 16, :]
    for one in leave:
        one.wait()


def split_kernel(place, parts, keep_ref, give_ref):
    h = place[1]
    total = parts[0].astype(F32)
    for i in range(1, 16):
        total = total + parts[i].astype(F32)
    keep_ref[...] = jnp.where(h == 0, total[0], total[1])
    give_ref[...] = jnp.where(h == 0, total[1], total[0])


def backward_kernel(
    place, w_h, slope_h, cot_h, prev_h, next_h, far_h, grad_ref,
    w_ref, slope, cot, cot_prev, cot_next, far, windows, sems,
):
    arrive = copies(
        sems, (w_h.at[SPACE:TAPS], w_ref.at[SPACE:TAPS]), (cot_h, cot), (prev_h, cot_prev), (next_h, cot_next),
        (far_h, far), (slope_h, slope), (w_h.at[0:SPACE], w_ref.at[0:SPACE]),
    )
    for one in arrive[:5]:
        one.wait()
    before, after = sides(place, cot_prev[...], cot_next[...], far[...])
    gh = dot_nt(after, tap(w_ref, 9))
    gh = gh + dot_nt(cot[...].astype(BF), tap(w_ref, 10))
    gh = gh + dot_nt(before, tap(w_ref, 11))
    arrive[5].wait()
    gs = (gh * slope[...]).astype(BF).astype(F32)
    fill_shifts(windows, gs)
    arrive[6].wait()
    acc = cot[...]
    for a in range(3):
        for b in range(3):
            acc = acc + dot_nt(windows[2 - b, (2 - a) * W : (2 - a) * W + ROWS, :], tap(w_ref, 3 * a + b))
    grad_ref[...] = acc


def middle_kernel(w_h, video_h, hidden_h, out_h, w_ref, video, hidden, out, sems):
    for one in copies(sems, (w_h.at[SPACE + 1], w_ref), (video_h, video), (hidden_h, hidden)):
        one.wait()
    out[...] = video[...] + dot(hidden[...], w_ref[...].reshape(C, C))
    for one in copies(sems, (out, out_h)):
        one.wait()


def output_kernel(
    place, w_h, part_h, prev_h, after_h, far_h, out_ref,
    w_ref, part, prev, after, far, sems,
):
    for one in copies(
        sems, (w_h.at[SPACE:TAPS], w_ref), (part_h, part), (prev_h, prev), (after_h, after), (far_h, far),
    ):
        one.wait()
    before, behind = sides(place, prev[...], after[...], far[...])
    acc = part[...] + dot(before, tap(w_ref, 0))
    out_ref[...] = acc + dot(behind, tap(w_ref, 2))


FRAME_B = (ROWS, C), BF
FRAME_F = (ROWS, C), F32
WINDOWS = (ROWS + 2 * W, 3 * C), BF
SHIFTS = (3, ROWS + 2 * W, C), BF
WEIGHTS = (TAPS, 2, HALF, C), BF
SUMS = (4, 4, 2, 16, C), F32
SHARE = (16, C), F32


def kernel_call(body, ins, outs, scratch, copied, micros, name, limit=60):
    spaces = {"s": pltpu.SMEM, "v": pltpu.VMEM, "h": pltpu.HBM}
    specs = [[pl.BlockSpec(memory_space=spaces[o[-1]]) for o in group] for group in (ins, outs)]
    return pl.pallas_call(
        body,
        out_shape=tuple(jax.ShapeDtypeStruct(*o[0]) for o in outs),
        in_specs=specs[0],
        out_specs=tuple(specs[1]),
        scratch_shapes=[pltpu.VMEM(*o) for o in scratch] + [pltpu.SemaphoreType.DMA((copied,))] * (copied > 0),
        compiler_params=pltpu.CompilerParams(vmem_limit_bytes=limit * 1024 * 1024),
        cost_estimate=pl.CostEstimate(flops=int(micros * 1.0e9), bytes_accessed=1_000_000, transcendentals=0),
        name=name,
    )(*(a for a, _ in ins))


def on_device(video, spatial_w, spatial_b, temporal_w, cotangent):
    tie = lax.optimization_barrier
    c, h, x, z = (lax.axis_index(a) for a in ("c", "h", "x", Z_LO))
    wrapped = ((z == 0) & (x > 0)) | ((z == 7) & (x < 3))
    place = jnp.stack([c, h, z, wrapped.astype(jnp.int32)]).astype(jnp.int32)
    shape = video.shape
    video_f = video.reshape(ROWS, C)
    cot_f = cotangent.reshape(ROWS, C)
    bias = spatial_b.reshape(1, C)

    cot_b = cot_f.astype(BF)
    w = jnp.concatenate([spatial_w, temporal_w.astype(BF)], axis=0)
    quarter = lax.dynamic_slice_in_dim(w, 3 * x, 3, 0).reshape(3 * OWN, C)
    other = across(jnp.pad(quarter, ((0, SLOT - 3 * OWN), (0, WIDE - C))))
    w = jnp.pad(w.reshape(TAPS * OWN, C), ((0, 0), (0, WIDE - C)))
    other, cot_b, w = tie((other, cot_b, w))
    far = lax.ppermute(cot_b, TM, FRAMES_FAR)
    cot_next = lax.ppermute(cot_b, TM, FRAMES_DOWN)
    cot_prev = lax.ppermute(cot_b, TM, FRAMES_UP)
    own_m = to_all(jnp.concatenate([w, other], axis=0), "y")
    (oth_m,) = kernel_call(
        apart_kernel, [(own_m, "v")], [(((4 * SLOT, WIDE), BF), "v")], [], 0, 1000, "apart", 8,
    )
    oth_m = lax.all_gather(oth_m, "x")
    oth_m, own_m, video_w = tie((oth_m, own_m, video_f))
    oth_m, cot_next, cot_prev, far = tie((oth_m, cot_next, cot_prev, far))
    (windows,) = kernel_call(prepare_kernel, [(video_w, "v")], [(WINDOWS, "v")], [], 0, 0.01, "prepare", 16)
    own_t, oth_t = core_swap(own_m), core_swap(oth_m)

    w_all, hidden, slope, mine, theirs = kernel_call(
        forward_kernel,
        [
            (place, "s"), (own_m, "v"), (own_t, "v"), (oth_m, "v"), (oth_t, "v"), (windows, "v"), (bias, "v"),
            (cot_f, "v"), (cot_prev, "v"), (cot_next, "v"), (far, "v"),
        ],
        [(WEIGHTS, "h"), (FRAME_B, "v"), (FRAME_F, "v"), (SUMS, "v"), (SUMS, "v")],
        [WEIGHTS], 1, 0.01, "forward", LIMIT,
    )
    part = (mine + core_swap(theirs)).astype(BF)
    part = lax.all_to_all(part.reshape(16, 2, 16, C), PLANE, 0, 0, tiled=True)
    prev = lax.ppermute(hidden, TM, FRAMES_UP)
    after = lax.ppermute(hidden, TM, FRAMES_DOWN)
    keep, give = kernel_call(
        split_kernel, [(place, "s"), (part, "v")], [(SHARE, "v"), (SHARE, "v")], [], 0, 1000, "split", 8,
    )
    give, hidden = tie((give, hidden))
    other = across(give)
    hidden_far = lax.ppermute(hidden, TM, FRAMES_FAR)
    (middle,) = kernel_call(
        middle_kernel, [(w_all, "h"), (video_f, "h"), (hidden, "h")], [(FRAME_F, "h")],
        [((2, HALF, C), BF), FRAME_F, FRAME_B, FRAME_F], 3, 1000, "middle",
    )
    other, middle, prev, after, slope = tie((other, middle, prev, after, slope))
    part = to_all((keep + other).astype(BF), Z_LO)
    (grad_video,) = kernel_call(
        backward_kernel,
        [(place, "s"), (w_all, "h"), (slope, "h"), (cot_f, "h"), (cot_prev, "h"), (cot_next, "h"), (far, "h")],
        [(FRAME_F, "v")],
        [WEIGHTS, FRAME_F, FRAME_F, FRAME_B, FRAME_B, FRAME_B, SHIFTS], 7, 0.01, "backward",
    )
    middle, grad_video, hidden_far = tie((middle, grad_video, hidden_far))
    (output,) = kernel_call(
        output_kernel,
        [(place, "s"), (w_all, "h"), (middle, "h"), (prev, "h"), (after, "h"), (hidden_far, "h")],
        [(FRAME_F, "v")],
        [((3, 2, HALF, C), BF), FRAME_F, FRAME_B, FRAME_B, FRAME_B], 5, 0.01, "output",
    )
    part, output = tie((part, output))
    part = part.astype(F32)
    part = jnp.sum(part, axis=0)
    part = to_all(part, "x").reshape(4 * 16, C)
    total_rows = ROWS * lax.axis_size(TM) * lax.axis_size(CLIP)
    grad_temporal = part[: 3 * OWN].reshape(3, OWN, C) * (1.0 / math.sqrt(total_rows))
    return output.reshape(shape), grad_video.reshape(shape), grad_temporal


def solution(mesh):
    finer = Mesh(mesh.devices.reshape(SIZES), AXES)
    placed = (
        P(CLIP, TM, None, None, None),
        P(None, CLIP, None),
        P(),
        P(None, CLIP, None),
        P(CLIP, TM, None, None, None),
    )
    return jax.shard_map(
        on_device,
        mesh=finer,
        in_specs=placed,
        out_specs=(
            P(CLIP, TM, None, None, None),
            P(CLIP, TM, None, None, None),
            P(None, CLIP, None),
        ),
        check_vma=False,
    )
```

```python
import math

import jax
import jax.numpy as jnp
from jax import lax
from jax.experimental import pallas as pl
from jax.experimental.pallas import tpu as pltpu
from jax.sharding import Mesh
from jax.sharding import PartitionSpec as P

AXES = ("x", "m", "k", "h", "y", "c")
SIZES = (4, 2, 4, 2, 4, 2)
TM = ("x", "m", "k")
Z_LO = ("m", "k")
CLIP = ("h", "y", "c")
PLANE = ("x", "y")
H, W, C = 16, 32, 320
ROWS = H * W
HALF, PART, OWN = 160, 40, 20
TAPS = 12
SPACE = 9
WIDE = 384
LIMIT = 48
SLOT = 64
BF = jnp.bfloat16
F32 = jnp.float32


def pairs_across():
    def place(z):
        return (z % 8) * 2 + z // 8

    there = [(z - 4) % 16 if z % 8 < 4 else (z + 4) % 16 for z in range(16)]
    return [(place(z), place(there[z])) for z in range(16)]


ACROSS = pairs_across()
FRAMES_UP = [(t, t + 1) for t in range(31) if t % 8 != 7]
FRAMES_DOWN = [(u, t) for t, u in FRAMES_UP]
FRAMES_FAR = [p for t in (7, 15, 23) for p in ((t, t + 1), (t + 1, t))]


def across(a):
    return lax.ppermute(a, ("m", "k", "h"), ACROSS)


def core_swap(a):
    return lax.ppermute(a, "c", [(0, 1), (1, 0)])


def to_all(a, axes):
    n = lax.axis_size(axes)
    return lax.all_to_all(jnp.broadcast_to(a[None], (n, *a.shape)), axes, 0, 0, tiled=True)


def dot(a, b):
    return lax.dot_general(a, b, (((1,), (0,)), ((), ())), preferred_element_type=F32)


def dot_nt(a, b):
    return lax.dot_general(a, b, (((1,), (1,)), ((), ())), preferred_element_type=F32)


def fill_windows(windows, value):
    col = lax.broadcasted_iota(jnp.int32, (ROWS, 1), 0) % W
    edge = jnp.zeros((W, 3 * C), BF)
    windows[0:W, :] = edge
    windows[W + ROWS : 2 * W + ROWS, :] = edge
    left = jnp.where(col == 0, 0.0, pltpu.roll(value, 1, 0))
    right = jnp.where(col == W - 1, 0.0, pltpu.roll(value, ROWS - 1, 0))
    windows[W : W + ROWS, :] = jnp.concatenate([a.astype(BF) for a in (left, value, right)], axis=1)


def fill_shifts(windows, value):
    col = lax.broadcasted_iota(jnp.int32, (ROWS, 1), 0) % W
    edge = jnp.zeros((W, C), BF)
    for d in range(3):
        windows[d, 0:W, :] = edge
        windows[d, W + ROWS : 2 * W + ROWS, :] = edge
    windows[1, W : W + ROWS, :] = value.astype(BF)
    left = jnp.where(col == 0, 0.0, pltpu.roll(value, 1, 0))
    windows[0, W : W + ROWS, :] = left.astype(BF)
    right = jnp.where(col == W - 1, 0.0, pltpu.roll(value, ROWS - 1, 0))
    windows[2, W : W + ROWS, :] = right.astype(BF)


def tap(w_ref, t):
    return w_ref[t].reshape(C, C)


def join(w_ref, t, half, y, mine, theirs, c):
    low = jnp.where(c == 0, mine, theirs)
    high = jnp.where(c == 0, theirs, mine)
    w_ref[t, half, y * PART : (y + 1) * PART, :] = jnp.concatenate([low, high], axis=0)


def sides(place, before, after, far):
    first, last = place[2] == 0, place[2] == 7
    return jnp.where(first, far, before), jnp.where(last, far, after)


def conv(windows, w_ref, bias):
    acc = jnp.zeros((ROWS, C), F32) + bias
    for a in range(3):
        acc = acc + dot(windows[a * W : a * W + ROWS, :], w_ref[3 * a : 3 * a + 3].reshape(3 * C, C))
    return acc


def copies(sems, *pairs):
    started = [pltpu.make_async_copy(src, dst, sems.at[i]) for i, (src, dst) in enumerate(pairs)]
    for one in started:
        one.start()
    return started


def prepare_kernel(video, windows):
    fill_windows(windows, video[...])


def apart_kernel(gathered, out):
    for y in range(4):
        out[y * SLOT : (y + 1) * SLOT, :] = gathered[y, TAPS * OWN : TAPS * OWN + SLOT, :]


def forward_kernel(
    place, own_m, own_t, oth_m, oth_t, windows, bias, cot, cot_prev, cot_next, far,
    w_h, hidden_ref, slope_ref, mine_ref, theirs_ref, w_ref, sems,
):
    c, h = place[0], place[1]
    for t in range(TAPS):
        for y in range(4):
            at = t * OWN
            join(w_ref, t, h, y, own_m[y, at : at + OWN, 0:C], own_t[y, at : at + OWN, 0:C], c)
            x, at = t // 3, y * SLOT + (t % 3) * OWN
            join(w_ref, t, 1 - h, y, oth_m[x, at : at + OWN, 0:C], oth_t[x, at : at + OWN, 0:C], c)
    leave = copies(sems, (w_ref, w_h))
    spatial = conv(windows, w_ref, bias[...])
    sig = jax.nn.sigmoid(spatial)
    hidden = (spatial * sig).astype(BF)
    hidden_ref[...] = hidden
    slope_ref[...] = sig * (1.0 + spatial * (1.0 - sig))
    before, after = sides(place, cot_prev[...], cot_next[...], far[...])
    turned = hidden.T
    grads = [dot(turned, other) for other in (after, cot[...].astype(BF), before)]
    pad = jnp.zeros((4, C), F32)
    for half in range(2):
        for y in range(4):
            both = []
            for core in range(2):
                r = half * HALF + y * PART + core * OWN
                both.append(jnp.concatenate([g[r : r + OWN, :] for g in grads] + [pad], axis=0))
            mine = jnp.where(c == 0, both[0], both[1])
            theirs = jnp.where(c == 0, both[1], both[0])
            for x in range(4):
                mine_ref[x, y, half] = mine[16 * x : 16 * x + 16, :]
                theirs_ref[x, y, half] = theirs[16 * x : 16 * x + 16, :]
    for one in leave:
        one.wait()


def split_kernel(place, parts, keep_ref, give_ref):
    h = place[1]
    total = parts[0].astype(F32)
    for i in range(1, 16):
        total = total + parts[i].astype(F32)
    keep_ref[...] = jnp.where(h == 0, total[0], total[1])
    give_ref[...] = jnp.where(h == 0, total[1], total[0])


def backward_kernel(
    place, w_h, slope_h, cot_h, prev_h, next_h, far_h, grad_ref,
    w_ref, slope, cot, cot_prev, cot_next, far, windows, sems,
):
    arrive = copies(
        sems, (w_h.at[SPACE:TAPS], w_ref.at[SPACE:TAPS]), (cot_h, cot), (prev_h, cot_prev), (next_h, cot_next),
        (far_h, far), (slope_h, slope), (w_h.at[0:SPACE], w_ref.at[0:SPACE]),
    )
    for one in arrive[:5]:
        one.wait()
    before, after = sides(place, cot_prev[...], cot_next[...], far[...])
    gh = dot_nt(after, tap(w_ref, 9))
    gh = gh + dot_nt(cot[...].astype(BF), tap(w_ref, 10))
    gh = gh + dot_nt(before, tap(w_ref, 11))
    arrive[5].wait()
    gs = (gh * slope[...]).astype(BF).astype(F32)
    fill_shifts(windows, gs)
    arrive[6].wait()
    acc = cot[...]
    for a in range(3):
        for b in range(3):
            acc = acc + dot_nt(windows[2 - b, (2 - a) * W : (2 - a) * W + ROWS, :], tap(w_ref, 3 * a + b))
    grad_ref[...] = acc


def middle_kernel(w_h, video_h, hidden_h, out_h, w_ref, video, hidden, out, sems):
    for one in copies(sems, (w_h.at[SPACE + 1], w_ref), (video_h, video), (hidden_h, hidden)):
        one.wait()
    out[...] = video[...] + dot(hidden[...], w_ref[...].reshape(C, C))
    for one in copies(sems, (out, out_h)):
        one.wait()


def output_kernel(
    place, w_h, part_h, prev_h, after_h, far_h, out_ref,
    w_ref, part, prev, after, far, sems,
):
    for one in copies(
        sems, (w_h.at[SPACE:TAPS], w_ref), (part_h, part), (prev_h, prev), (after_h, after), (far_h, far),
    ):
        one.wait()
    before, behind = sides(place, prev[...], after[...], far[...])
    acc = part[...] + dot(before, tap(w_ref, 0))
    out_ref[...] = acc + dot(behind, tap(w_ref, 2))


FRAME_B = (ROWS, C), BF
FRAME_F = (ROWS, C), F32
WINDOWS = (ROWS + 2 * W, 3 * C), BF
SHIFTS = (3, ROWS + 2 * W, C), BF
WEIGHTS = (TAPS, 2, HALF, C), BF
SUMS = (4, 4, 2, 16, C), F32
SHARE = (16, C), F32


def kernel_call(body, ins, outs, scratch, copied, micros, name, limit=60):
    spaces = {"s": pltpu.SMEM, "v": pltpu.VMEM, "h": pltpu.HBM}
    specs = [[pl.BlockSpec(memory_space=spaces[o[-1]]) for o in group] for group in (ins, outs)]
    return pl.pallas_call(
        body,
        out_shape=tuple(jax.ShapeDtypeStruct(*o[0]) for o in outs),
        in_specs=specs[0],
        out_specs=tuple(specs[1]),
        scratch_shapes=[pltpu.VMEM(*o) for o in scratch] + [pltpu.SemaphoreType.DMA((copied,))] * (copied > 0),
        compiler_params=pltpu.CompilerParams(vmem_limit_bytes=limit * 1024 * 1024),
        cost_estimate=pl.CostEstimate(flops=int(micros * 1.0e9), bytes_accessed=1_000_000, transcendentals=0),
        name=name,
    )(*(a for a, _ in ins))


def on_device(video, spatial_w, spatial_b, temporal_w, cotangent):
    tie = lax.optimization_barrier
    c, h, x, z = (lax.axis_index(a) for a in ("c", "h", "x", Z_LO))
    wrapped = ((z == 0) & (x > 0)) | ((z == 7) & (x < 3))
    place = jnp.stack([c, h, z, wrapped.astype(jnp.int32)]).astype(jnp.int32)
    shape = video.shape
    video_f = video.reshape(ROWS, C)
    cot_f = cotangent.reshape(ROWS, C)
    bias = spatial_b.reshape(1, C)

    cot_b = cot_f.astype(BF)
    w = jnp.concatenate([spatial_w, temporal_w.astype(BF)], axis=0)
    quarter = lax.dynamic_slice_in_dim(w, 3 * x, 3, 0).reshape(3 * OWN, C)
    other = across(jnp.pad(quarter, ((0, SLOT - 3 * OWN), (0, WIDE - C))))
    w = jnp.pad(w.reshape(TAPS * OWN, C), ((0, 0), (0, WIDE - C)))
    other, cot_b, w = tie((other, cot_b, w))
    far = lax.ppermute(cot_b, TM, FRAMES_FAR)
    cot_next = lax.ppermute(cot_b, TM, FRAMES_DOWN)
    cot_prev = lax.ppermute(cot_b, TM, FRAMES_UP)
    own_m = to_all(jnp.concatenate([w, other], axis=0), "y")
    (oth_m,) = kernel_call(
        apart_kernel, [(own_m, "v")], [(((4 * SLOT, WIDE), BF), "v")], [], 0, 1000, "apart", 8,
    )
    oth_m = lax.all_gather(oth_m, "x")
    oth_m, own_m, video_w = tie((oth_m, own_m, video_f))
    oth_m, cot_next, cot_prev, far = tie((oth_m, cot_next, cot_prev, far))
    (windows,) = kernel_call(prepare_kernel, [(video_w, "v")], [(WINDOWS, "v")], [], 0, 0.01, "prepare", 16)
    own_t, oth_t = core_swap(own_m), core_swap(oth_m)

    w_all, hidden, slope, mine, theirs = kernel_call(
        forward_kernel,
        [
            (place, "s"), (own_m, "v"), (own_t, "v"), (oth_m, "v"), (oth_t, "v"), (windows, "v"), (bias, "v"),
            (cot_f, "v"), (cot_prev, "v"), (cot_next, "v"), (far, "v"),
        ],
        [(WEIGHTS, "h"), (FRAME_B, "v"), (FRAME_F, "v"), (SUMS, "v"), (SUMS, "v")],
        [WEIGHTS], 1, 0.01, "forward", LIMIT,
    )
    part = (mine + core_swap(theirs)).astype(BF)
    part = lax.all_to_all(part.reshape(16, 2, 16, C), PLANE, 0, 0, tiled=True)
    prev = lax.ppermute(hidden, TM, FRAMES_UP)
    after = lax.ppermute(hidden, TM, FRAMES_DOWN)
    (grad_video,) = kernel_call(
        backward_kernel,
        [(place, "s"), (w_all, "h"), (slope, "h"), (cot_f, "h"), (cot_prev, "h"), (cot_next, "h"), (far, "h")],
        [(FRAME_F, "v")],
        [WEIGHTS, FRAME_F, FRAME_F, FRAME_B, FRAME_B, FRAME_B, SHIFTS], 7, 0.01, "backward", 44,
    )
    part, grad_video = tie((part, grad_video))
    keep, give = kernel_call(
        split_kernel, [(place, "s"), (part, "v")], [(SHARE, "v"), (SHARE, "v")], [], 0, 1000, "split", 8,
    )
    give, hidden = tie((give, hidden))
    other = across(give)
    hidden_far = lax.ppermute(hidden, TM, FRAMES_FAR)
    (middle,) = kernel_call(
        middle_kernel, [(w_all, "h"), (video_f, "h"), (hidden, "h")], [(FRAME_F, "h")],
        [((2, HALF, C), BF), FRAME_F, FRAME_B, FRAME_F], 3, 1000, "middle",
    )
    other, middle, prev, after = tie((other, middle, prev, after))
    part = to_all((keep + other).astype(BF), Z_LO)
    (output,) = kernel_call(
        output_kernel,
        [(place, "s"), (w_all, "h"), (middle, "h"), (prev, "h"), (after, "h"), (hidden_far, "h")],
        [(FRAME_F, "v")],
        [((3, 2, HALF, C), BF), FRAME_F, FRAME_B, FRAME_B, FRAME_B], 5, 0.01, "output",
    )
    part, output = tie((part, output))
    part = part.astype(F32)
    part = jnp.sum(part, axis=0)
    part = to_all(part, "x").reshape(4 * 16, C)
    total_rows = ROWS * lax.axis_size(TM) * lax.axis_size(CLIP)
    grad_temporal = part[: 3 * OWN].reshape(3, OWN, C) * (1.0 / math.sqrt(total_rows))
    return output.reshape(shape), grad_video.reshape(shape), grad_temporal


def solution(mesh):
    finer = Mesh(mesh.devices.reshape(SIZES), AXES)
    placed = (
        P(CLIP, TM, None, None, None),
        P(None, CLIP, None),
        P(),
        P(None, CLIP, None),
        P(CLIP, TM, None, None, None),
    )
    return jax.shard_map(
        on_device,
        mesh=finer,
        in_specs=placed,
        out_specs=(
            P(CLIP, TM, None, None, None),
            P(CLIP, TM, None, None, None),
            P(None, CLIP, None),
        ),
        check_vma=False,
    )
```

```python
import math

import jax
import jax.numpy as jnp
from jax import lax
from jax.experimental import pallas as pl
from jax.experimental.pallas import tpu as pltpu
from jax.sharding import Mesh
from jax.sharding import PartitionSpec as P

AXES = ("x", "m", "k", "h", "y", "c")
SIZES = (4, 2, 4, 2, 4, 2)
TM = ("x", "m", "k")
Z_LO = ("m", "k")
CLIP = ("h", "y", "c")
PLANE = ("x", "y")
H, W, C = 16, 32, 320
ROWS = H * W
HALF, PART, OWN = 160, 40, 20
TAPS = 12
SPACE = 9
WIDE = 384
LIMIT = 48
SLOT = 64
BF = jnp.bfloat16
F32 = jnp.float32


def pairs_across():
    def place(z):
        return (z % 8) * 2 + z // 8

    there = [(z - 4) % 16 if z % 8 < 4 else (z + 4) % 16 for z in range(16)]
    return [(place(z), place(there[z])) for z in range(16)]


ACROSS = pairs_across()
FRAMES_UP = [(t, t + 1) for t in range(31) if t % 8 != 7]
FRAMES_DOWN = [(u, t) for t, u in FRAMES_UP]
FRAMES_FAR = [p for t in (7, 15, 23) for p in ((t, t + 1), (t + 1, t))]


def across(a):
    return lax.ppermute(a, ("m", "k", "h"), ACROSS)


def core_swap(a):
    return lax.ppermute(a, "c", [(0, 1), (1, 0)])


def to_all(a, axes):
    n = lax.axis_size(axes)
    return lax.all_to_all(jnp.broadcast_to(a[None], (n, *a.shape)), axes, 0, 0, tiled=True)


def dot(a, b):
    return lax.dot_general(a, b, (((1,), (0,)), ((), ())), preferred_element_type=F32)


def dot_nt(a, b):
    return lax.dot_general(a, b, (((1,), (1,)), ((), ())), preferred_element_type=F32)


def fill_windows(windows, value):
    col = lax.broadcasted_iota(jnp.int32, (ROWS, 1), 0) % W
    edge = jnp.zeros((W, 3 * C), BF)
    windows[0:W, :] = edge
    windows[W + ROWS : 2 * W + ROWS, :] = edge
    left = jnp.where(col == 0, 0.0, pltpu.roll(value, 1, 0))
    right = jnp.where(col == W - 1, 0.0, pltpu.roll(value, ROWS - 1, 0))
    windows[W : W + ROWS, :] = jnp.concatenate([a.astype(BF) for a in (left, value, right)], axis=1)


def fill_shifts(windows, value):
    col = lax.broadcasted_iota(jnp.int32, (ROWS, 1), 0) % W
    edge = jnp.zeros((W, C), BF)
    for d in range(3):
        windows[d, 0:W, :] = edge
        windows[d, W + ROWS : 2 * W + ROWS, :] = edge
    windows[1, W : W + ROWS, :] = value.astype(BF)
    left = jnp.where(col == 0, 0.0, pltpu.roll(value, 1, 0))
    windows[0, W : W + ROWS, :] = left.astype(BF)
    right = jnp.where(col == W - 1, 0.0, pltpu.roll(value, ROWS - 1, 0))
    windows[2, W : W + ROWS, :] = right.astype(BF)


def tap(w_ref, t):
    return w_ref[t].reshape(C, C)


def join(w_ref, t, half, y, mine, theirs, c):
    low = jnp.where(c == 0, mine, theirs)
    high = jnp.where(c == 0, theirs, mine)
    w_ref[t, half, y * PART : (y + 1) * PART, :] = jnp.concatenate([low, high], axis=0)


def sides(place, before, after, far):
    first, last = place[2] == 0, place[2] == 7
    return jnp.where(first, far, before), jnp.where(last, far, after)


def conv(windows, w_ref, bias):
    acc = jnp.zeros((ROWS, C), F32) + bias
    for a in range(3):
        acc = acc + dot(windows[a * W : a * W + ROWS, :], w_ref[3 * a : 3 * a + 3].reshape(3 * C, C))
    return acc


def copies(sems, *pairs):
    started = [pltpu.make_async_copy(src, dst, sems.at[i]) for i, (src, dst) in enumerate(pairs)]
    for one in started:
        one.start()
    return started


def prepare_kernel(video, windows):
    fill_windows(windows, video[...])


def apart_kernel(gathered, out):
    for y in range(4):
        out[y * SLOT : (y + 1) * SLOT, :] = gathered[y, TAPS * OWN : TAPS * OWN + SLOT, :]


def forward_kernel(
    place, own_m, own_t, oth_m, oth_t, windows, bias, cot, cot_prev, cot_next, far,
    w_h, hidden_ref, slope_ref, mine_ref, theirs_ref, w_ref, sems,
):
    c, h = place[0], place[1]
    for t in range(TAPS):
        for y in range(4):
            at = t * OWN
            join(w_ref, t, h, y, own_m[y, at : at + OWN, 0:C], own_t[y, at : at + OWN, 0:C], c)
            x, at = t // 3, y * SLOT + (t % 3) * OWN
            join(w_ref, t, 1 - h, y, oth_m[x, at : at + OWN, 0:C], oth_t[x, at : at + OWN, 0:C], c)
    leave = copies(sems, (w_ref, w_h))
    spatial = conv(windows, w_ref, bias[...])
    sig = jax.nn.sigmoid(spatial)
    hidden = (spatial * sig).astype(BF)
    hidden_ref[...] = hidden
    slope_ref[...] = sig * (1.0 + spatial * (1.0 - sig))
    before, after = sides(place, cot_prev[...], cot_next[...], far[...])
    turned = hidden.T
    grads = [dot(turned, other) for other in (after, cot[...].astype(BF), before)]
    pad = jnp.zeros((4, C), F32)
    for half in range(2):
        for y in range(4):
            both = []
            for core in range(2):
                r = half * HALF + y * PART + core * OWN
                both.append(jnp.concatenate([g[r : r + OWN, :] for g in grads] + [pad], axis=0))
            mine = jnp.where(c == 0, both[0], both[1])
            theirs = jnp.where(c == 0, both[1], both[0])
            for x in range(4):
                mine_ref[x, y, half] = mine[16 * x : 16 * x + 16, :]
                theirs_ref[x, y, half] = theirs[16 * x : 16 * x + 16, :]
    for one in leave:
        one.wait()


def split_kernel(place, parts, total_ref, give_ref):
    total = parts[0].astype(F32)
    for i in range(1, 16):
        total = total + parts[i].astype(F32)
    total_ref[...] = total
    give_ref[...] = jnp.where(place[1] == 0, total[1], total[0])


def keep_kernel(place, total, keep_ref):
    keep_ref[...] = jnp.where(place[1] == 0, total[0], total[1])


def backward_kernel(
    place, w_h, slope_h, cot_h, prev_h, next_h, far_h, grad_ref,
    w_ref, slope, cot, cot_prev, cot_next, far, windows, sems,
):
    arrive = copies(
        sems, (w_h.at[SPACE:TAPS], w_ref.at[SPACE:TAPS]), (cot_h, cot), (prev_h, cot_prev), (next_h, cot_next),
        (far_h, far), (slope_h, slope), (w_h.at[0:SPACE], w_ref.at[0:SPACE]),
    )
    for one in arrive[:5]:
        one.wait()
    before, after = sides(place, cot_prev[...], cot_next[...], far[...])
    gh = dot_nt(after, tap(w_ref, 9))
    gh = gh + dot_nt(cot[...].astype(BF), tap(w_ref, 10))
    gh = gh + dot_nt(before, tap(w_ref, 11))
    arrive[5].wait()
    gs = (gh * slope[...]).astype(BF).astype(F32)
    fill_shifts(windows, gs)
    arrive[6].wait()
    acc = cot[...]
    for a in range(3):
        for b in range(3):
            acc = acc + dot_nt(windows[2 - b, (2 - a) * W : (2 - a) * W + ROWS, :], tap(w_ref, 3 * a + b))
    grad_ref[...] = acc


def output_kernel(
    place, w_h, video_h, hidden_h, prev_h, after_h, far_h, out_ref,
    w_ref, video, hidden, prev, after, far, sems,
):
    for one in copies(
        sems, (w_h.at[SPACE:TAPS], w_ref), (video_h, video), (hidden_h, hidden), (prev_h, prev), (after_h, after), (far_h, far),
    ):
        one.wait()
    before, behind = sides(place, prev[...], after[...], far[...])
    acc = video[...] + dot(hidden[...], tap(w_ref, 1))
    acc = acc + dot(before, tap(w_ref, 0))
    out_ref[...] = acc + dot(behind, tap(w_ref, 2))


FRAME_B = (ROWS, C), BF
FRAME_F = (ROWS, C), F32
WINDOWS = (ROWS + 2 * W, 3 * C), BF
SHIFTS = (3, ROWS + 2 * W, C), BF
WEIGHTS = (TAPS, 2, HALF, C), BF
SUMS = (4, 4, 2, 16, C), F32
SHARE = (16, C), F32


def kernel_call(body, ins, outs, scratch, copied, micros, name, limit=60):
    spaces = {"s": pltpu.SMEM, "v": pltpu.VMEM, "h": pltpu.HBM}
    specs = [[pl.BlockSpec(memory_space=spaces[o[-1]]) for o in group] for group in (ins, outs)]
    return pl.pallas_call(
        body,
        out_shape=tuple(jax.ShapeDtypeStruct(*o[0]) for o in outs),
        in_specs=specs[0],
        out_specs=tuple(specs[1]),
        scratch_shapes=[pltpu.VMEM(*o) for o in scratch] + [pltpu.SemaphoreType.DMA((copied,))] * (copied > 0),
        compiler_params=pltpu.CompilerParams(vmem_limit_bytes=limit * 1024 * 1024),
        cost_estimate=pl.CostEstimate(flops=int(micros * 1.0e9), bytes_accessed=1_000_000, transcendentals=0),
        name=name,
    )(*(a for a, _ in ins))


def on_device(video, spatial_w, spatial_b, temporal_w, cotangent):
    tie = lax.optimization_barrier
    c, h, x, z = (lax.axis_index(a) for a in ("c", "h", "x", Z_LO))
    wrapped = ((z == 0) & (x > 0)) | ((z == 7) & (x < 3))
    place = jnp.stack([c, h, z, wrapped.astype(jnp.int32)]).astype(jnp.int32)
    shape = video.shape
    video_f = video.reshape(ROWS, C)
    cot_f = cotangent.reshape(ROWS, C)
    bias = spatial_b.reshape(1, C)

    cot_b = cot_f.astype(BF)
    w = jnp.concatenate([spatial_w, temporal_w.astype(BF)], axis=0)
    quarter = lax.dynamic_slice_in_dim(w, 3 * x, 3, 0).reshape(3 * OWN, C)
    other = across(jnp.pad(quarter, ((0, SLOT - 3 * OWN), (0, WIDE - C))))
    w = jnp.pad(w.reshape(TAPS * OWN, C), ((0, 0), (0, WIDE - C)))
    other, cot_b, w = tie((other, cot_b, w))
    far = lax.ppermute(cot_b, TM, FRAMES_FAR)
    cot_next = lax.ppermute(cot_b, TM, FRAMES_DOWN)
    cot_prev = lax.ppermute(cot_b, TM, FRAMES_UP)
    own_m = to_all(jnp.concatenate([w, other], axis=0), "y")
    (oth_m,) = kernel_call(
        apart_kernel, [(own_m, "v")], [(((4 * SLOT, WIDE), BF), "v")], [], 0, 1000, "apart", 8,
    )
    oth_m = lax.all_gather(oth_m, "x")
    oth_m, own_m, video_w = tie((oth_m, own_m, video_f))
    oth_m, cot_next, cot_prev, far = tie((oth_m, cot_next, cot_prev, far))
    (windows,) = kernel_call(prepare_kernel, [(video_w, "v")], [(WINDOWS, "v")], [], 0, 0.01, "prepare", 16)
    own_t, oth_t = core_swap(own_m), core_swap(oth_m)

    w_all, hidden, slope, mine, theirs = kernel_call(
        forward_kernel,
        [
            (place, "s"), (own_m, "v"), (own_t, "v"), (oth_m, "v"), (oth_t, "v"), (windows, "v"), (bias, "v"),
            (cot_f, "v"), (cot_prev, "v"), (cot_next, "v"), (far, "v"),
        ],
        [(WEIGHTS, "h"), (FRAME_B, "v"), (FRAME_F, "v"), (SUMS, "v"), (SUMS, "v")],
        [WEIGHTS], 1, 0.01, "forward", LIMIT,
    )
    part = (mine + core_swap(theirs)).astype(BF)
    part = lax.all_to_all(part.reshape(16, 2, 16, C), PLANE, 0, 0, tiled=True)
    prev = lax.ppermute(hidden, TM, FRAMES_UP)
    after = lax.ppermute(hidden, TM, FRAMES_DOWN)
    total, give = kernel_call(
        split_kernel, [(place, "s"), (part, "v")], [(((2, 16, C), F32), "v"), (SHARE, "v")], [], 0, 1000, "split", 8,
    )
    give, total, hidden = tie((give, total, hidden))
    other = across(give)
    hidden_far = lax.ppermute(hidden, TM, FRAMES_FAR)
    (keep,) = kernel_call(keep_kernel, [(place, "s"), (total, "v")], [(SHARE, "v")], [], 0, 1000, "keep", 8)
    other, keep, prev, after, slope, video_f = tie((other, keep, prev, after, slope, video_f))
    part = to_all((keep + other).astype(BF), Z_LO)
    (grad_video,) = kernel_call(
        backward_kernel,
        [(place, "s"), (w_all, "h"), (slope, "h"), (cot_f, "h"), (cot_prev, "h"), (cot_next, "h"), (far, "h")],
        [(FRAME_F, "v")],
        [WEIGHTS, FRAME_F, FRAME_F, FRAME_B, FRAME_B, FRAME_B, SHIFTS], 7, 0.01, "backward",
    )
    video_f, grad_video, hidden_far = tie((video_f, grad_video, hidden_far))
    (output,) = kernel_call(
        output_kernel,
        [(place, "s"), (w_all, "h"), (video_f, "h"), (hidden, "h"), (prev, "h"), (after, "h"), (hidden_far, "h")],
        [(FRAME_F, "v")],
        [((3, 2, HALF, C), BF), FRAME_F, FRAME_B, FRAME_B, FRAME_B, FRAME_B], 6, 0.01, "output",
    )
    part, output = tie((part, output))
    part = part.astype(F32)
    part = jnp.sum(part, axis=0)
    part = to_all(part, "x").reshape(4 * 16, C)
    total_rows = ROWS * lax.axis_size(TM) * lax.axis_size(CLIP)
    grad_temporal = part[: 3 * OWN].reshape(3, OWN, C) * (1.0 / math.sqrt(total_rows))
    return output.reshape(shape), grad_video.reshape(shape), grad_temporal


def solution(mesh):
    finer = Mesh(mesh.devices.reshape(SIZES), AXES)
    placed = (
        P(CLIP, TM, None, None, None),
        P(None, CLIP, None),
        P(),
        P(None, CLIP, None),
        P(CLIP, TM, None, None, None),
    )
    return jax.shard_map(
        on_device,
        mesh=finer,
        in_specs=placed,
        out_specs=(
            P(CLIP, TM, None, None, None),
            P(CLIP, TM, None, None, None),
            P(None, CLIP, None),
        ),
        check_vma=False,
    )
```

```python
import math

import jax
import jax.numpy as jnp
from jax import lax
from jax.experimental import pallas as pl
from jax.experimental.pallas import tpu as pltpu
from jax.sharding import Mesh
from jax.sharding import PartitionSpec as P

AXES = ("x", "m", "k", "h", "y", "c")
SIZES = (4, 2, 4, 2, 4, 2)
TM = ("x", "m", "k")
Z_LO = ("m", "k")
CLIP = ("h", "y", "c")
PLANE = ("x", "y")
H, W, C = 16, 32, 320
ROWS = H * W
HALF, PART, OWN = 160, 40, 20
TAPS = 12
SPACE = 9
WIDE = 384
LIMIT = 48
SLOT = 64
BF = jnp.bfloat16
F32 = jnp.float32


def pairs_across():
    def place(z):
        return (z % 8) * 2 + z // 8

    there = [(z - 4) % 16 if z % 8 < 4 else (z + 4) % 16 for z in range(16)]
    return [(place(z), place(there[z])) for z in range(16)]


ACROSS = pairs_across()
FRAMES_UP = [(t, t + 1) for t in range(31) if t % 8 != 7]
FRAMES_DOWN = [(u, t) for t, u in FRAMES_UP]
FRAMES_FAR = [p for t in (7, 15, 23) for p in ((t, t + 1), (t + 1, t))]


def across(a):
    return lax.ppermute(a, ("m", "k", "h"), ACROSS)


def core_swap(a):
    return lax.ppermute(a, "c", [(0, 1), (1, 0)])


def to_all(a, axes):
    n = lax.axis_size(axes)
    return lax.all_to_all(jnp.broadcast_to(a[None], (n, *a.shape)), axes, 0, 0, tiled=True)


def dot(a, b):
    return lax.dot_general(a, b, (((1,), (0,)), ((), ())), preferred_element_type=F32)


def dot_nt(a, b):
    return lax.dot_general(a, b, (((1,), (1,)), ((), ())), preferred_element_type=F32)


def fill_windows(windows, value):
    col = lax.broadcasted_iota(jnp.int32, (ROWS, 1), 0) % W
    edge = jnp.zeros((W, 3 * C), BF)
    windows[0:W, :] = edge
    windows[W + ROWS : 2 * W + ROWS, :] = edge
    left = jnp.where(col == 0, 0.0, pltpu.roll(value, 1, 0))
    right = jnp.where(col == W - 1, 0.0, pltpu.roll(value, ROWS - 1, 0))
    windows[W : W + ROWS, :] = jnp.concatenate([a.astype(BF) for a in (left, value, right)], axis=1)


def fill_shifts(windows, value):
    col = lax.broadcasted_iota(jnp.int32, (ROWS, 1), 0) % W
    edge = jnp.zeros((W, C), BF)
    for d in range(3):
        windows[d, 0:W, :] = edge
        windows[d, W + ROWS : 2 * W + ROWS, :] = edge
    windows[1, W : W + ROWS, :] = value.astype(BF)
    left = jnp.where(col == 0, 0.0, pltpu.roll(value, 1, 0))
    windows[0, W : W + ROWS, :] = left.astype(BF)
    right = jnp.where(col == W - 1, 0.0, pltpu.roll(value, ROWS - 1, 0))
    windows[2, W : W + ROWS, :] = right.astype(BF)


def tap(w_ref, t):
    return w_ref[t].reshape(C, C)


def join(w_ref, t, half, y, mine, theirs, c):
    low = jnp.where(c == 0, mine, theirs)
    high = jnp.where(c == 0, theirs, mine)
    w_ref[t, half, y * PART : (y + 1) * PART, :] = jnp.concatenate([low, high], axis=0)


def sides(place, before, after, far):
    first, last = place[2] == 0, place[2] == 7
    return jnp.where(first, far, before), jnp.where(last, far, after)


def conv(windows, w_ref, bias):
    acc = jnp.zeros((ROWS, C), F32) + bias
    for a in range(3):
        acc = acc + dot(windows[a * W : a * W + ROWS, :], w_ref[3 * a : 3 * a + 3].reshape(3 * C, C))
    return acc


def copies(sems, *pairs):
    started = [pltpu.make_async_copy(src, dst, sems.at[i]) for i, (src, dst) in enumerate(pairs)]
    for one in started:
        one.start()
    return started


def prepare_kernel(video, windows):
    fill_windows(windows, video[...])


def apart_kernel(gathered, out):
    for y in range(4):
        out[y * SLOT : (y + 1) * SLOT, :] = gathered[y, TAPS * OWN : TAPS * OWN + SLOT, :]


def forward_kernel(
    place, own_m, own_t, oth_m, oth_t, windows, bias, cot, cot_prev, cot_next, far,
    w_h, hidden_ref, slope_ref, mine_ref, theirs_ref, w_ref, sems,
):
    c, h = place[0], place[1]
    for t in range(TAPS):
        for y in range(4):
            at = t * OWN
            join(w_ref, t, h, y, own_m[y, at : at + OWN, 0:C], own_t[y, at : at + OWN, 0:C], c)
            x, at = t // 3, y * SLOT + (t % 3) * OWN
            join(w_ref, t, 1 - h, y, oth_m[x, at : at + OWN, 0:C], oth_t[x, at : at + OWN, 0:C], c)
    leave = copies(sems, (w_ref, w_h))
    spatial = conv(windows, w_ref, bias[...])
    sig = jax.nn.sigmoid(spatial)
    hidden = (spatial * sig).astype(BF)
    hidden_ref[...] = hidden
    slope_ref[...] = sig * (1.0 + spatial * (1.0 - sig))
    before, after = sides(place, cot_prev[...], cot_next[...], far[...])
    turned = hidden.T
    grads = [dot(turned, other) for other in (after, cot[...].astype(BF), before)]
    pad = jnp.zeros((4, C), F32)
    for half in range(2):
        for y in range(4):
            both = []
            for core in range(2):
                r = half * HALF + y * PART + core * OWN
                both.append(jnp.concatenate([g[r : r + OWN, :] for g in grads] + [pad], axis=0))
            mine = jnp.where(c == 0, both[0], both[1])
            theirs = jnp.where(c == 0, both[1], both[0])
            for x in range(4):
                mine_ref[x, y, half] = mine[16 * x : 16 * x + 16, :]
                theirs_ref[x, y, half] = theirs[16 * x : 16 * x + 16, :]
    for one in leave:
        one.wait()


def split_kernel(place, parts, total_ref, give_ref):
    total = parts[0].astype(F32)
    for i in range(1, 16):
        total = total + parts[i].astype(F32)
    total_ref[...] = total
    give_ref[...] = jnp.where(place[1] == 0, total[1], total[0])


def keep_kernel(place, total, keep_ref):
    keep_ref[...] = jnp.where(place[1] == 0, total[0], total[1])


def backward_kernel(
    place, w_h, slope_h, cot_h, prev_h, next_h, far_h, grad_ref,
    w_ref, slope, cot, cot_prev, cot_next, far, windows, sems,
):
    arrive = copies(
        sems, (w_h.at[SPACE:TAPS], w_ref.at[SPACE:TAPS]), (cot_h, cot), (prev_h, cot_prev), (next_h, cot_next),
        (far_h, far), (slope_h, slope), (w_h.at[0:SPACE], w_ref.at[0:SPACE]),
    )
    for one in arrive[:5]:
        one.wait()
    before, after = sides(place, cot_prev[...], cot_next[...], far[...])
    gh = dot_nt(after, tap(w_ref, 9))
    gh = gh + dot_nt(cot[...].astype(BF), tap(w_ref, 10))
    gh = gh + dot_nt(before, tap(w_ref, 11))
    arrive[5].wait()
    gs = (gh * slope[...]).astype(BF).astype(F32)
    fill_shifts(windows, gs)
    arrive[6].wait()
    acc = cot[...]
    for a in range(3):
        for b in range(3):
            acc = acc + dot_nt(windows[2 - b, (2 - a) * W : (2 - a) * W + ROWS, :], tap(w_ref, 3 * a + b))
    grad_ref[...] = acc


def output_kernel(
    place, w_h, video_h, hidden_h, prev_h, after_h, far_h, out_ref,
    w_ref, video, hidden, prev, after, far, sems,
):
    for one in copies(
        sems, (w_h.at[SPACE:TAPS], w_ref), (video_h, video), (hidden_h, hidden), (prev_h, prev), (after_h, after), (far_h, far),
    ):
        one.wait()
    before, behind = sides(place, prev[...], after[...], far[...])
    acc = video[...] + dot(hidden[...], tap(w_ref, 1))
    acc = acc + dot(before, tap(w_ref, 0))
    out_ref[...] = acc + dot(behind, tap(w_ref, 2))


FRAME_B = (ROWS, C), BF
FRAME_F = (ROWS, C), F32
WINDOWS = (ROWS + 2 * W, 3 * C), BF
SHIFTS = (3, ROWS + 2 * W, C), BF
WEIGHTS = (TAPS, 2, HALF, C), BF
SUMS = (4, 4, 2, 16, C), F32
SHARE = (16, C), F32


def kernel_call(body, ins, outs, scratch, copied, micros, name, limit=60):
    spaces = {"s": pltpu.SMEM, "v": pltpu.VMEM, "h": pltpu.HBM}
    specs = [[pl.BlockSpec(memory_space=spaces[o[-1]]) for o in group] for group in (ins, outs)]
    return pl.pallas_call(
        body,
        out_shape=tuple(jax.ShapeDtypeStruct(*o[0]) for o in outs),
        in_specs=specs[0],
        out_specs=tuple(specs[1]),
        scratch_shapes=[pltpu.VMEM(*o) for o in scratch] + [pltpu.SemaphoreType.DMA((copied,))] * (copied > 0),
        compiler_params=pltpu.CompilerParams(vmem_limit_bytes=limit * 1024 * 1024),
        cost_estimate=pl.CostEstimate(flops=int(micros * 1.0e9), bytes_accessed=1_000_000, transcendentals=0),
        name=name,
    )(*(a for a, _ in ins))


def on_device(video, spatial_w, spatial_b, temporal_w, cotangent):
    tie = lax.optimization_barrier
    c, h, x, z = (lax.axis_index(a) for a in ("c", "h", "x", Z_LO))
    wrapped = ((z == 0) & (x > 0)) | ((z == 7) & (x < 3))
    place = jnp.stack([c, h, z, wrapped.astype(jnp.int32)]).astype(jnp.int32)
    shape = video.shape
    video_f = video.reshape(ROWS, C)
    cot_f = cotangent.reshape(ROWS, C)
    bias = spatial_b.reshape(1, C)

    cot_b = cot_f.astype(BF)
    w = jnp.concatenate([spatial_w, temporal_w.astype(BF)], axis=0)
    quarter = lax.dynamic_slice_in_dim(w, 3 * x, 3, 0).reshape(3 * OWN, C)
    other = across(jnp.pad(quarter, ((0, SLOT - 3 * OWN), (0, WIDE - C))))
    w = jnp.pad(w.reshape(TAPS * OWN, C), ((0, 0), (0, WIDE - C)))
    other, cot_b, w = tie((other, cot_b, w))
    far = lax.ppermute(cot_b, TM, FRAMES_FAR)
    cot_next = lax.ppermute(cot_b, TM, FRAMES_DOWN)
    cot_prev = lax.ppermute(cot_b, TM, FRAMES_UP)
    own_m = to_all(jnp.concatenate([w, other], axis=0), "y")
    (oth_m,) = kernel_call(
        apart_kernel, [(own_m, "v")], [(((4 * SLOT, WIDE), BF), "v")], [], 0, 1000, "apart", 8,
    )
    oth_m = lax.all_gather(oth_m, "x")
    oth_m, own_m, video_w = tie((oth_m, own_m, video_f))
    oth_m, cot_next, cot_prev, far = tie((oth_m, cot_next, cot_prev, far))
    (windows,) = kernel_call(prepare_kernel, [(video_w, "v")], [(WINDOWS, "v")], [], 0, 0.01, "prepare", 16)
    own_t, oth_t = core_swap(own_m), core_swap(oth_m)

    w_all, hidden, slope, mine, theirs = kernel_call(
        forward_kernel,
        [
            (place, "s"), (own_m, "v"), (own_t, "v"), (oth_m, "v"), (oth_t, "v"), (windows, "v"), (bias, "v"),
            (cot_f, "v"), (cot_prev, "v"), (cot_next, "v"), (far, "v"),
        ],
        [(WEIGHTS, "h"), (FRAME_B, "v"), (FRAME_F, "v"), (SUMS, "v"), (SUMS, "v")],
        [WEIGHTS], 1, 0.01, "forward", LIMIT,
    )
    part = (mine + core_swap(theirs)).astype(BF)
    part = lax.all_to_all(part.reshape(16, 2, 16, C), PLANE, 0, 0, tiled=True)
    prev = lax.ppermute(hidden, TM, FRAMES_UP)
    after = lax.ppermute(hidden, TM, FRAMES_DOWN)
    total, give = kernel_call(
        split_kernel, [(place, "s"), (part, "v")], [(((2, 16, C), F32), "v"), (SHARE, "v")], [], 0, 1000, "split", 8,
    )
    give, total, hidden = tie((give, total, hidden))
    other = across(give)
    hidden_far = lax.ppermute(hidden, TM, FRAMES_FAR)
    (keep,) = kernel_call(keep_kernel, [(place, "s"), (total, "v")], [(SHARE, "v")], [], 0, 1000, "keep", 8)
    other, keep, prev, after, slope, video_f = tie((other, keep, prev, after, slope, video_f))
    part = to_all((keep + other).astype(BF), Z_LO)
    (grad_video,) = kernel_call(
        backward_kernel,
        [(place, "s"), (w_all, "h"), (slope, "h"), (cot_f, "h"), (cot_prev, "h"), (cot_next, "h"), (far, "h")],
        [(FRAME_F, "v")],
        [WEIGHTS, FRAME_F, FRAME_F, FRAME_B, FRAME_B, FRAME_B, SHIFTS], 7, 0.01, "backward",
    )
    video_f, grad_video, hidden_far = tie((video_f, grad_video, hidden_far))
    (output,) = kernel_call(
        output_kernel,
        [(place, "s"), (w_all, "h"), (video_f, "h"), (hidden, "h"), (prev, "h"), (after, "h"), (hidden_far, "h")],
        [(FRAME_F, "v")],
        [((3, 2, HALF, C), BF), FRAME_F, FRAME_B, FRAME_B, FRAME_B, FRAME_B], 6, 0.01, "output", 40,
    )
    part, output = tie((part, output))
    part = part.astype(F32)
    part = jnp.sum(part, axis=0)
    part = to_all(part, "x").reshape(4 * 16, C)
    total_rows = ROWS * lax.axis_size(TM) * lax.axis_size(CLIP)
    grad_temporal = part[: 3 * OWN].reshape(3, OWN, C) * (1.0 / math.sqrt(total_rows))
    return output.reshape(shape), grad_video.reshape(shape), grad_temporal


def solution(mesh):
    finer = Mesh(mesh.devices.reshape(SIZES), AXES)
    placed = (
        P(CLIP, TM, None, None, None),
        P(None, CLIP, None),
        P(),
        P(None, CLIP, None),
        P(CLIP, TM, None, None, None),
    )
    return jax.shard_map(
        on_device,
        mesh=finer,
        in_specs=placed,
        out_specs=(
            P(CLIP, TM, None, None, None),
            P(CLIP, TM, None, None, None),
            P(None, CLIP, None),
        ),
        check_vma=False,
    )
```
